256 devices in a mesh: head: 16 (over y, x_lo, core), key: 16 (over x_hi, z).
Axes of the slice: x: 4 (x_hi: 2, x_lo: 2; x = x_hi * 2 + x_lo), y: 4, z: 8, core: 2. Of those that a mesh axis runs over, the one named last changes fastest.
Arguments:
- queries: bfloat16 [128, 128, 192], P(None, 'head'), may hold values from -16 to 16
- w_uk: bfloat16 [128, 128, 512], P('head'), may hold values from -0.5 to 0.5
- w_uv: bfloat16 [128, 512, 128], P('head'), may hold values from -0.25 to 0.25
- latent: bfloat16 [32768, 576], P('key'), may hold values from -5 to 5
- out_grad: bfloat16 [128, 128, 128], P(None, 'head'), may hold values from -6 to 6
- offsets: int32 [128], replicated, may hold values from 8192 to 32767, as said below
Outputs:
- d_queries: bfloat16 [128, 128, 192], P('key', 'head')
- d_latent: bfloat16 [32768, 576], P('key')
The draws below stay inside these ranges and needn't reach their ends.
Inputs may be any that keep to these rules, and one draw needn't show every extreme that they name: Row r sees keys 0 to offsets[r].
All inputs are finite; a program needn't handle non-finite values.
Results may differ from the reference program's by a relative error of at most 0.0079.
Values may be sent and summed in bfloat16 or wider, within the bound.
No kernel may reach another device: no remote copies, remote signals or barrier semaphores. Data moves between devices by JAX's collectives and lax.ppermute only.
A program may use at most 128 MiB of HBM per device.

```python
import math
import jax
import jax.numpy as jnp
from jax import lax

H = 128
DN = 128
DR = 64
DC = 512
DV = 128
R = 128
S = 32768


def draw_queries(key, part):
    inner = jax.random.fold_in(key, 11)
    base = jnp.clip(jax.random.normal(inner, (R, H, DN + DR), jnp.float32), -4.0, 4.0)
    return base.astype(jnp.bfloat16)


def draw_latent(key, part):
    inner = jax.random.fold_in(key, 13)
    fraction = jnp.arange(S, dtype=jnp.float32) / S
    base = jnp.clip(jax.random.normal(inner, (S, DC + DR), jnp.float32), -4.0, 4.0) * (0.75 + 0.5 * fraction)[:, None]
    return base.astype(jnp.bfloat16)


def draw_offsets(key, part):
    inner = jax.random.fold_in(key, 17)
    first, second = jax.random.split(inner)
    values = jax.random.randint(first, (R,), S // 4, S)
    order = jax.random.permutation(second, R)
    return values.at[order[0]].set(S - 1).at[order[1]].set(S // 4)


def steps_of(key, shape, shards, smallest, high):
    loudness = 1.0
    for position, shards_of in shards:
        steps = jax.random.uniform(jax.random.fold_in(jax.random.fold_in(key, 6), position), (shards_of,), jnp.float32, smallest / len(shards), high / len(shards))
        loudness = loudness * jnp.repeat(jnp.exp(steps), shape[position] // shards_of).reshape((-1,) + (1,) * (len(shape) - 1 - position))
    return loudness


def centred(key, dims, deviation, most, pieces=(), kind=jnp.bfloat16):
    loudness = steps_of(key, dims, pieces, -0.22, 0.18) if pieces else 1.0
    result = jax.random.normal(key, dims, jnp.float32) * deviation * loudness
    return jnp.minimum(jnp.maximum(result, -most), most).astype(kind)


def setup_inputs(seed: int = 0) -> dict:
    splits = jax.random.split(jax.random.key(seed), 7)
    queries = draw_queries(jax.random.fold_in(splits[6], 71), 0)
    w_uk = centred(splits[1], (H, DN, DC), DN ** -0.5, 0.5, ((0, 16),))
    w_uv = centred(splits[2], (H, DC, DV), DC ** -0.5, 0.25, ((0, 16),))
    latent = draw_latent(jax.random.fold_in(splits[6], 71), 0)
    out_grad = centred(splits[4], (R, H, DV), 1.0, 6.0, ((1, 16),))
    offsets = draw_offsets(jax.random.fold_in(splits[6], 71), 0)
    return dict(queries=queries, w_uk=w_uk, w_uv=w_uv, latent=latent, out_grad=out_grad, offsets=offsets)


floor_score = -1e+30

def reference(queries, w_uk, w_uv, latent, out_grad, offsets):
    scale = 1.0 / math.sqrt(DN + DR)
    visible = jnp.arange(S, dtype=jnp.int32)[None, :] <= offsets[:, None]
    values = latent[:, :DC]

    def per_head(carry, inputs):
        q_head, up_key, up_value, grad = inputs
        q_lat = jnp.dot(q_head[:, :DN], up_key, preferred_element_type=jnp.float32).astype(jnp.bfloat16)
        q_cat = jnp.concatenate([q_lat, q_head[:, DN:]], axis=1)
        d_lat = jnp.dot(grad, up_value.T, preferred_element_type=jnp.float32).astype(jnp.bfloat16)
        scores = jnp.dot(q_cat, latent.T, preferred_element_type=jnp.float32) * scale
        scores = jnp.where(visible, scores, floor_score)
        top = lax.optimization_barrier(jnp.max(scores, axis=1))
        total = lax.optimization_barrier(jnp.sum(jnp.where(visible, jnp.exp(scores - top[:, None]), 0.0), axis=1))
        log_norm = top + jnp.log(total)
        probs = jnp.where(visible, jnp.exp(scores - log_norm[:, None]), 0.0)
        d_probs = jnp.dot(d_lat, values.T, preferred_element_type=jnp.float32)
        delta = lax.optimization_barrier(jnp.sum(probs * d_probs, axis=1))
        d_scores = (probs * (d_probs - delta[:, None])).astype(jnp.bfloat16)
        dq_lat = jnp.dot(d_scores, latent, preferred_element_type=jnp.float32) * scale
        dq_nope = jnp.dot(dq_lat[:, :DC], up_key.astype(jnp.float32).T, precision=lax.Precision.HIGHEST)
        dq_head = jnp.concatenate([dq_nope, dq_lat[:, DC:]], axis=1).astype(jnp.bfloat16)
        from_scores = jnp.dot(d_scores.T, q_cat, preferred_element_type=jnp.float32) * scale
        from_values = jnp.dot(probs.astype(jnp.bfloat16).T, d_lat, preferred_element_type=jnp.float32)
        carry = carry + jnp.concatenate([from_scores[:, :DC] + from_values, from_scores[:, DC:]], axis=1)
        return (carry, dq_head)
    start = jnp.zeros((S, DC + DR), jnp.float32)
    summed, dq_all = lax.scan(per_head, start, (jnp.transpose(queries, (1, 0, 2)), w_uk, w_uv, jnp.transpose(out_grad, (1, 0, 2))))
    return (jnp.transpose(dq_all, (1, 0, 2)), summed.astype(jnp.bfloat16))
```

```python
import functools
import math

import jax
import jax.numpy as jnp
from jax import lax
from jax.experimental import pallas as pl
from jax.experimental.pallas import tpu as pltpu
from jax.sharding import PartitionSpec as P

bf16 = jnp.bfloat16
f32 = jnp.float32
floor_score = -1e30
floor_top = -1e20

HEADS = 8
ROWS = 128
NOPE = 128
ROT = 64
LAT = 512
WIDE = LAT + ROT
KEYS = 2048
BLK = 256
NBLK = KEYS // BLK
ALL = HEADS * ROWS
PEERS = 16
PART = WIDE // 3
HALF = PART // 2
SCALE = 1.0 / math.sqrt(NOPE + ROT)
SCALE2 = SCALE * math.log2(math.e)
VLIM = 60 * 1024 * 1024

NT = (((1,), (1,)), ((), ()))


def dot(a, b):
    return jnp.dot(a, b, preferred_element_type=f32)


def dot_nt(a, b):
    return lax.dot_general(a, b, NT, preferred_element_type=f32)


def params(limit=VLIM):
    return pltpu.CompilerParams(vmem_limit_bytes=limit)


def whole(shape):
    return pl.BlockSpec(shape, lambda *_: (0,) * len(shape))


KB1 = 2
CHUNK = 256


def pass_one(
    sc, off, qt, wuk, wuv, og, lat, e_out, dp_out, qcat, dlat, stat, s_scr, top, tot, dsum, offc
):
    i = pl.program_id(0)
    steps = NBLK // KB1

    @pl.when(i == 0)
    def _():
        offc[...] = jnp.broadcast_to(off[...], (ROWS, ROWS)).T - sc[0]
        for h in range(HEADS):
            rows = slice(h * ROWS, (h + 1) * ROWS)
            q = qt[h].T
            qcat[rows, :LAT] = dot(q[:, :NOPE], wuk[h]).astype(bf16)
            qcat[rows, LAT:] = q[:, NOPE:]
            dlat[rows, :] = dot_nt(og[h], wuv[h]).astype(bf16)
        top[...] = jnp.full((ALL, 128), floor_top, f32)
        tot[...] = jnp.zeros((ALL, 128), f32)
        dsum[...] = jnp.zeros((ALL, 128), f32)

    @pl.when(i < steps)
    def _():
        lane = lax.broadcasted_iota(jnp.int32, (ROWS, BLK), 1)
        for j in range(KB1):
            cols = slice(j * BLK, (j + 1) * BLK)
            at = lane + (i * KB1 + j) * BLK
            bound = jnp.concatenate([offc[...]] * (BLK // 128), axis=1)
            seen = at <= bound
            for c in range(ALL // CHUNK):
                rows = slice(c * CHUNK, (c + 1) * CHUNK)
                s = dot(qcat[rows, :], lat[:, cols]) * SCALE2
                s = jnp.where(jnp.concatenate([seen] * (CHUNK // ROWS), axis=0), s, floor_score)
                s_scr[i * KB1 + j, rows, :] = s
                best = top[rows, :]
                for k in range(BLK // 128):
                    best = jnp.maximum(best, s[:, k * 128 : (k + 1) * 128])
                top[rows, :] = best

    @pl.when(i == steps - 1)
    def _():
        top[...] = jnp.broadcast_to(jnp.max(top[...], axis=1, keepdims=True), (ALL, 128))

    @pl.when(i >= steps)
    def _():
        for j in range(KB1):
            cols = slice(j * BLK, (j + 1) * BLK)
            for c in range(ALL // CHUNK):
                rows = slice(c * CHUNK, (c + 1) * CHUNK)
                dp = dot(dlat[rows, :], lat[:LAT, cols])
                dp_out[j, rows, :] = dp
                s = s_scr[(i - steps) * KB1 + j, rows, :]
                m = top[rows, :]
                t, d = tot[rows, :], dsum[rows, :]
                for k in range(BLK // 128):
                    lanes = slice(k * 128, (k + 1) * 128)
                    e = jnp.exp2(s[:, lanes] - m)
                    e_out[j, rows, lanes] = e
                    t = t + e
                    d = d + e * dp[:, lanes]
                tot[rows, :] = t
                dsum[rows, :] = d

    @pl.when(i == 2 * steps - 1)
    def _():
        lane = lax.broadcasted_iota(jnp.int32, (ROWS, 128), 1)
        for h in range(HEADS):
            rows = slice(h * ROWS, (h + 1) * ROWS)
            t = jnp.sum(tot[rows, :], axis=1, keepdims=True)
            d = jnp.sum(dsum[rows, :], axis=1, keepdims=True)
            x = jnp.where(lane == 0, top[rows, :], jnp.where(lane == 1, t, d)).T
            for k in range(3):
                line = x[k : k + 1, :]
                for peer in range(PEERS):
                    stat[peer, k * 8 + h : k * 8 + h + 1, :] = line


def run_pass_one(base, offsets, qt, wuk, wuv, og, lat_t):
    steps = NBLK // KB1
    out_block = lambda i, sc: (jnp.maximum(i - steps, 0), 0, 0)
    return pl.pallas_call(
        pass_one,
        grid_spec=pltpu.PrefetchScalarGridSpec(
            num_scalar_prefetch=1,
            grid=(2 * steps,),
            in_specs=[
                whole((1, ROWS)),
                whole(qt.shape),
                whole(wuk.shape),
                whole(wuv.shape),
                whole(og.shape),
                pl.BlockSpec((WIDE, KB1 * BLK), lambda i, sc: (0, lax.rem(i, steps))),
            ],
            out_specs=[
                pl.BlockSpec((KB1, ALL, BLK), out_block),
                pl.BlockSpec((KB1, ALL, BLK), out_block),
                whole((ALL, WIDE)),
                whole((ALL, LAT)),
                whole((PEERS, 24, 128)),
            ],
            scratch_shapes=[
                pltpu.VMEM((NBLK, ALL, BLK), f32),
                pltpu.VMEM((ALL, 128), f32),
                pltpu.VMEM((ALL, 128), f32),
                pltpu.VMEM((ALL, 128), f32),
                pltpu.VMEM((ROWS, 128), jnp.int32),
            ],
        ),
        out_shape=[
            jax.ShapeDtypeStruct((NBLK, ALL, BLK), f32),
            jax.ShapeDtypeStruct((NBLK, ALL, BLK), f32),
            jax.ShapeDtypeStruct((ALL, WIDE), bf16),
            jax.ShapeDtypeStruct((ALL, LAT), bf16),
            jax.ShapeDtypeStruct((PEERS, 24, 128), f32),
        ],
        compiler_params=params(),
        name="pass_one",
    )(base, offsets, qt, wuk, wuv, og, lat_t)


def turn(qcat, dlat, qcat_t, dlat_t):
    for h in range(HEADS):
        rows = slice(h * ROWS, (h + 1) * ROWS)
        for k in range(LAT // 128):
            lanes = slice(k * 128, (k + 1) * 128)
            qcat_t[lanes, rows] = qcat[rows, lanes].T
            dlat_t[lanes, rows] = dlat[rows, lanes].T
        qcat_t[LAT:, rows] = qcat[rows, LAT:].T


def run_turn(qcat, dlat):
    return pl.pallas_call(
        turn,
        out_shape=[
            jax.ShapeDtypeStruct((WIDE, ALL), bf16),
            jax.ShapeDtypeStruct((LAT, ALL), bf16),
        ],
        compiler_params=params(),
        name="turn",
    )(qcat, dlat)


def place(p, r):
    order = [r[p % 3], r[(p + 1) % 3], r[(p + 2) % 3]]
    return order[0] * 4 + order[1] * 2 + order[2]


def second_core(sc, e, dp, qcat_t, dlat_t, coef, delta, x_out, ds_out, pb):
    i = pl.program_id(0)
    for c in range(ALL // CHUNK):
        rows = slice(c * CHUNK, (c + 1) * CHUNK)
        cf, dl = coef[rows, :], delta[rows, :]
        for k in range(BLK // 128):
            lanes = slice(k * 128, (k + 1) * 128)
            p = e[0, rows, lanes] * cf
            pb[rows, lanes] = p.astype(bf16)
            ds_out[0, rows, lanes] = (p * (dp[0, rows, lanes] - dl)).astype(bf16)
    scores = dot(qcat_t[...], ds_out[0]) * SCALE
    values = dot(dlat_t[...], pb[...])
    low = (scores[:LAT] + values).astype(bf16)
    high = scores[LAT:].astype(bf16)
    r0, r1 = lax.rem(i, 2), lax.div(i, 2)
    for p in range(3):
        for h in range(2):
            at = place(p, (r0, r1, jnp.bitwise_xor(sc[2], h)))
            first = p * PART + h * HALF
            if first + HALF <= LAT:
                block = low[first : first + HALF]
            elif first >= LAT:
                block = high[first - LAT : first - LAT + HALF]
            else:
                block = jnp.concatenate([low[first:], high[: first + HALF - LAT]], axis=0)
            x_out[p, at] = block


def second_first(sc, stat, e, dp, qcat_t, dlat_t, x_out, ds_out, coef, delta, pb):
    @pl.when(pl.program_id(0) == 0)
    def _():
        m = stat[:, 0:8, :]
        best = jnp.max(m, axis=0)
        w = jnp.exp2(m - best[None])
        total = jnp.sum(w * stat[:, 8:16, :], axis=0)
        dtotal = jnp.sum(w * stat[:, 16:24, :], axis=0)
        cf = jnp.exp2(stat[sc[4], 0:8, :] - best) / total
        dl = dtotal / total
        for h in range(HEADS):
            rows = slice(h * ROWS, (h + 1) * ROWS)
            coef[rows, :] = jnp.broadcast_to(cf[h : h + 1], (128, 128)).T
            delta[rows, :] = jnp.broadcast_to(dl[h : h + 1], (128, 128)).T

    second_core(sc, e, dp, qcat_t, dlat_t, coef, delta, x_out, ds_out, pb)


def second_later(sc, coef, delta, e, dp, qcat_t, dlat_t, x_out, ds_out, pb):
    second_core(sc, e, dp, qcat_t, dlat_t, coef, delta, x_out, ds_out, pb)


def key_block(i, sc):
    a0 = jnp.bitwise_xor(lax.rem(i, 2), sc[0])
    a1 = jnp.bitwise_xor(lax.div(i, 2), sc[1])
    return sc[3] * 4 + a1 * 2 + a0


def run_second(sc, heads_in, e, dp, qcat_t, dlat_t, first):
    block = pl.BlockSpec((1, ALL, BLK), lambda i, sc: (key_block(i, sc), 0, 0))
    column = jax.ShapeDtypeStruct((ALL, 128), f32)
    outs = [
        jax.ShapeDtypeStruct((3, 8, HALF, BLK), bf16),
        jax.ShapeDtypeStruct((4, ALL, BLK), bf16),
    ]
    specs = [whole((3, 8, HALF, BLK)), pl.BlockSpec((1, ALL, BLK), lambda i, sc: (i, 0, 0))]
    if first:
        outs += [column, column]
        specs += [whole(column.shape)] * 2
    return pl.pallas_call(
        second_first if first else second_later,
        grid_spec=pltpu.PrefetchScalarGridSpec(
            num_scalar_prefetch=1,
            grid=(4,),
            in_specs=[whole(a.shape) for a in heads_in]
            + [block, block, whole(qcat_t.shape), whole(dlat_t.shape)],
            out_specs=specs,
            scratch_shapes=[pltpu.VMEM((ALL, BLK), bf16)],
        ),
        out_shape=outs,
        compiler_params=params(),
        name="second_first" if first else "second_later",
    )(sc, *heads_in, e, dp, qcat_t, dlat_t)


def query_grad(sc_a, sc_b, ds_a, ds_b, lat_a, lat_b, wuk, keep, send, acc, wide):
    i = pl.program_id(0)
    part = dot_nt(ds_a[0], lat_a[...]) + dot_nt(ds_b[0], lat_b[...])

    @pl.when(i == 0)
    def _():
        acc[...] = part

    @pl.when(i > 0)
    def _():
        acc[...] += part

    @pl.when(i == 3)
    def _():
        for h in range(HEADS):
            rows = slice(h * ROWS, (h + 1) * ROWS)
            x = acc[rows, :LAT] * SCALE
            hi = x.astype(bf16)
            lo = (x - hi.astype(f32)).astype(bf16)
            wide[h, :, :NOPE] = dot_nt(hi, wuk[h]) + dot_nt(lo, wuk[h])
            wide[h, :, NOPE:] = acc[rows, LAT:] * SCALE
        for g in range(PEERS):
            bits = (g >> 3 & 1) | (g >> 2 & 1) << 1 | (g >> 1 & 1) << 2 | (g & 1) << 3
            owner = jnp.bitwise_xor(sc_a[4], bits)
            mine = wide[:, pl.ds(pl.multiple_of(owner * 8, 8), 8), :]
            block = mine.reshape(HEADS * 8, NOPE + ROT).astype(bf16)
            if g < 8:
                keep[g] = block
            else:
                send[g - 8] = block


def run_query_grad(sc_a, sc_b, ds_a, ds_b, lat_t, wuk):
    half = jax.ShapeDtypeStruct((8, HEADS * 8, NOPE + ROT), bf16)
    step = pl.BlockSpec((1, ALL, BLK), lambda i, a, b: (i, 0, 0))
    return pl.pallas_call(
        query_grad,
        grid_spec=pltpu.PrefetchScalarGridSpec(
            num_scalar_prefetch=2,
            grid=(4,),
            in_specs=[
                step,
                step,
                pl.BlockSpec((WIDE, BLK), lambda i, a, b: (0, key_block(i, a))),
                pl.BlockSpec((WIDE, BLK), lambda i, a, b: (0, key_block(i, b))),
                whole(wuk.shape),
            ],
            out_specs=[whole(half.shape)] * 2,
            scratch_shapes=[
                pltpu.VMEM((ALL, WIDE), f32),
                pltpu.VMEM((HEADS, ROWS, NOPE + ROT), f32),
            ],
        ),
        out_shape=[half, half],
        compiler_params=params(),
        name="query_grad",
    )(sc_a, sc_b, ds_a, ds_b, lat_t, lat_t, wuk)


def halve(single, *refs):
    kept, got = refs[0], refs[1 : 2 if single else 4]
    outs = refs[2 if single else 4 :]
    for p in range(3):
        n = kept.shape[1]
        for k in range(n):
            other = got[0][p, k] if single else got[p][k]
            total = (kept[p, k].astype(f32) + other.astype(f32)).astype(bf16)
            if n == 1:
                outs[p][0] = total
            elif k < n // 2:
                outs[0][p, k] = total
            else:
                outs[1 + p][k - n // 2] = total


def run_halve(kept, got):
    n = kept.shape[1]
    one = lambda k: jax.ShapeDtypeStruct((k, HALF, BLK), bf16)
    if n == 1:
        outs = [one(1)] * 3
    else:
        outs = [jax.ShapeDtypeStruct((3, n // 2, HALF, BLK), bf16)] + [one(n // 2)] * 3
    return pl.pallas_call(
        functools.partial(halve, len(got) == 1),
        out_shape=outs,
        compiler_params=params(),
        name="halve",
    )(kept, *got)


def join(last, *refs):
    n = refs[0].shape[0]
    for p in range(3):
        for src, at in ((refs[p], 0), (refs[3 + p], n)):
            refs[6 + p][at : at + n] = src[...]
            if last:
                refs[9][p, at : at + n] = src[...]


def run_join(own, got, last):
    n = 2 * own[0].shape[0]
    outs = [jax.ShapeDtypeStruct((n, HALF, BLK), bf16)] * 3
    if last:
        outs = outs + [jax.ShapeDtypeStruct((3, n, HALF, BLK), bf16)]
    return pl.pallas_call(
        functools.partial(join, last),
        out_shape=outs,
        compiler_params=params(),
        name="join",
    )(*own, *got)


def settle(sc, *refs):
    mine, mine_far, other, other_far, out = refs[0], refs[1:4], refs[4], refs[5:8], refs[8]
    for near, far, half in ((mine, mine_far, sc[3]), (other, other_far, 1 - sc[3])):
        for p in range(3):
            for i in range(8):
                r = [0, 0, 0]
                r[p % 3], r[(p + 1) % 3], r[(p + 2) % 3] = i >> 2 & 1, i >> 1 & 1, i & 1
                a = [jnp.bitwise_xor(sc[d], r[d]) for d in range(3)]
                rows = pl.ds(pl.multiple_of(p * PART + a[2] * HALF, 32), HALF)
                lanes = pl.ds(pl.multiple_of((half * 4 + a[1] * 2 + a[0]) * BLK, BLK), BLK)
                out[rows, lanes] = near[p, i] if i < 4 else far[p][i - 4]


def run_settle(sc, *pieces):
    return pl.pallas_call(
        settle,
        grid_spec=pltpu.PrefetchScalarGridSpec(
            num_scalar_prefetch=1,
            grid=(1,),
            in_specs=[whole(a.shape) for a in pieces],
            out_specs=whole((WIDE, KEYS)),
        ),
        out_shape=jax.ShapeDtypeStruct((WIDE, KEYS), bf16),
        compiler_params=params(),
        name="settle",
    )(sc, *pieces)


def cube_neighbour(k, d):
    y, rest = k >> 2, k & 3
    if d == 2:
        return k ^ 2
    gray = (y ^ (y >> 1)) ^ (1 << d)
    back = gray ^ (gray >> 1)
    return back * 4 + rest


def along(value, d):
    return lax.ppermute(value, "head", [(k, cube_neighbour(k, d)) for k in range(16)])


def to_sibling(value):
    return lax.ppermute(value, "head", [(k, k ^ 1) for k in range(16)])


def shards(queries, w_uk, w_uv, latent, out_grad, offsets):
    head = lax.axis_index("head").astype(jnp.int32)
    key = lax.axis_index("key").astype(jnp.int32)
    y = head >> 2
    gray = y ^ (y >> 1)
    core = head & 1
    sc_own = jnp.stack([gray & 1, gray >> 1, (head >> 1) & 1, core, key])
    sc_far = jnp.stack([gray & 1, gray >> 1, (head >> 1) & 1, 1 - core, key])
    lat_t = latent.T
    qt = jnp.transpose(queries, (1, 2, 0))
    og = jnp.transpose(out_grad, (1, 0, 2))
    e, dp, qcat, dlat, stat = run_pass_one(
        (key * KEYS)[None], offsets[None], qt, w_uk, w_uv, og, lat_t
    )
    stat = lax.all_to_all(stat, "key", 0, 0, tiled=True)
    qcat_t, dlat_t = run_turn(qcat, dlat)
    x_far, ds_far, coef, delta = run_second(sc_far, (stat,), e, dp, qcat_t, dlat_t, True)
    came = to_sibling(x_far)
    x_own, ds_own = run_second(sc_own, (coef, delta), e, dp, qcat_t, dlat_t, False)
    kept, *send = run_halve(x_own, [came])
    for step in range(3):
        got = [along(send[p], (p + step) % 3) for p in range(3)]
        if step == 0:
            q_keep, q_send = run_query_grad(sc_far, sc_own, ds_far, ds_own, lat_t, w_uk)
        kept, *send = run_halve(kept, got) if step < 2 else (None, *run_halve(kept, got))
    own = send
    for step in range(2):
        got = [along(own[p], (p + 2 - step) % 3) for p in range(3)]
        own = run_join(own, got, step == 1)
    near = own[3]
    far = [along(own[p], p) for p in range(3)]
    near_other = to_sibling(near)
    far_other = [to_sibling(a) for a in far]
    d_latent = run_settle(sc_own, near, *far, near_other, *far_other).T

    for flip in (1, 2, 4, 8):
        got = lax.ppermute(q_send, "key", [(k, k ^ flip) for k in range(16)])
        total = (q_keep.astype(f32) + got.astype(f32)).astype(bf16)
        n = total.shape[0] // 2
        q_keep, q_send = (total[:n], total[n:]) if n else (total, None)
    d_queries = jnp.transpose(q_keep[0].reshape(HEADS, 8, NOPE + ROT), (1, 0, 2))
    return (d_queries, d_latent)


def solution(mesh):
    return jax.shard_map(
        shards,
        mesh=mesh,
        in_specs=(
            P(None, "head", None),
            P("head", None, None),
            P("head", None, None),
            P("key", None),
            P(None, "head", None),
            P(),
        ),
        out_specs=(P("key", "head", None), P("key", None)),
        check_vma=False,
    )
```

```python
import functools
import math

import jax
import jax.numpy as jnp
from jax import lax
from jax.experimental import pallas as pl
from jax.experimental.pallas import tpu as pltpu
from jax.sharding import PartitionSpec as P

bf16 = jnp.bfloat16
f32 = jnp.float32
floor_score = -1e30
floor_top = -1e20

HEADS = 8
ROWS = 128
NOPE = 128
ROT = 64
LAT = 512
WIDE = LAT + ROT
KEYS = 2048
BLK = 256
NBLK = KEYS // BLK
ALL = HEADS * ROWS
PEERS = 16
COLS = WIDE // 2
SCALE = 1.0 / math.sqrt(NOPE + ROT)
SCALE2 = SCALE * math.log2(math.e)
VLIM = 12 * 1024 * 1024

NT = (((1,), (1,)), ((), ()))


def dot(a, b):
    return jnp.dot(a, b, preferred_element_type=f32)


def dot_nt(a, b):
    return lax.dot_general(a, b, NT, preferred_element_type=f32)


def params(limit=VLIM):
    return pltpu.CompilerParams(vmem_limit_bytes=limit)


in_vmem = pl.BlockSpec(memory_space=pltpu.VMEM)
in_hbm = pl.BlockSpec(memory_space=pltpu.HBM)
in_smem = pl.BlockSpec(memory_space=pltpu.SMEM)


def call(kernel, name, outs, args, scalars=0, scratch=(), limit=VLIM):
    return pl.pallas_call(
        kernel,
        in_specs=[in_smem] * scalars + [in_vmem] * (len(args) - scalars),
        out_specs=[in_vmem] * len(outs),
        out_shape=[jax.ShapeDtypeStruct(shape, kind) for shape, kind in outs],
        scratch_shapes=list(scratch),
        compiler_params=params(limit),
        name=name,
    )(*args)


CHUNK = 256


def pass_one(
    base, off, qt, wuk, wuv, og, lat,
    e_out, dp_out, qcat_out, dlat_out, stat,
    qt_v, wuk_v, wuv_v, og_v, lat_v, og_wide, qcat, dlat, e_v, dp_v, top, tot, dsum, hide,
    sem_in, sem_e, sem_dp, sem_q,
):
    pairs = ((qt, qt_v), (wuk, wuk_v), (og, og_v), (wuv, wuv_v), (lat, lat_v))
    loads = [pltpu.make_async_copy(a, b, sem_in.at[k]) for k, (a, b) in enumerate(pairs)]
    for copy in loads:
        copy.start()
    bound = jnp.broadcast_to(off[...], (ROWS, ROWS)).T - base[0]
    bound = jnp.concatenate([bound] * (BLK // 128), axis=1)
    lane = lax.broadcasted_iota(jnp.int32, (ROWS, BLK), 1)
    top[...] = jnp.full((ALL, 128), floor_top, f32)
    tot[...] = jnp.zeros((ALL, 128), f32)
    dsum[...] = jnp.zeros((ALL, 128), f32)
    chunks = [slice(c * CHUNK, (c + 1) * CHUNK) for c in range(ALL // CHUNK)]
    heads = [slice(h * ROWS, (h + 1) * ROWS) for h in range(HEADS)]

    loads[0].wait()
    loads[1].wait()
    for h, rows in enumerate(heads):
        q = qt_v[h].T
        qcat[rows, :LAT] = dot(q[:, :NOPE], wuk_v[h]).astype(bf16)
        qcat[rows, LAT:] = q[:, NOPE:]
    loads[2].wait()
    loads[3].wait()
    og_wide[...] = og_v[...].astype(f32)
    for h, rows in enumerate(heads):
        grad = og_wide[pl.ds(h, ROWS, stride=HEADS), :].astype(bf16)
        dlat[rows, :] = dot_nt(grad, wuv_v[h]).astype(bf16)
    loads[4].wait()
    saves = [
        pltpu.make_async_copy(qcat, qcat_out, sem_q.at[0]),
        pltpu.make_async_copy(dlat, dlat_out, sem_q.at[1]),
    ]
    for copy in saves:
        copy.start()

    def score(j, _):
        at = pl.multiple_of(j * BLK, BLK)
        hide[...] = jnp.where(lane + at <= bound, 0.0, floor_score)
        cols = lat_v[:, pl.ds(at, BLK)]
        for rows in chunks:
            s = dot(qcat[rows, :], cols)
            s = (s.reshape(CHUNK // ROWS, ROWS, BLK) + hide[...][None]).reshape(CHUNK, BLK)
            e_v[j, rows, :] = s
            best = top[rows, :]
            for k in range(BLK // 128):
                best = jnp.maximum(best, s[:, k * 128 : (k + 1) * 128])
            top[rows, :] = best
        return 0

    lax.fori_loop(0, NBLK, score, 0)
    top[...] = jnp.broadcast_to(jnp.max(top[...], axis=1, keepdims=True) * SCALE2, (ALL, 128))

    def outgoing(j):
        return (
            pltpu.make_async_copy(e_v.at[j], e_out.at[j], sem_e.at[j]),
            pltpu.make_async_copy(dp_v.at[j], dp_out.at[j], sem_dp.at[j]),
        )

    def weigh(j, _):
        cols = lat_v[:LAT, pl.ds(pl.multiple_of(j * BLK, BLK), BLK)]
        for rows in chunks:
            dp = dot(dlat[rows, :], cols)
            dp_v[j, rows, :] = dp
            s = e_v[j, rows, :]
            m = top[rows, :]
            t, d = tot[rows, :], dsum[rows, :]
            for k in range(BLK // 128):
                lanes = slice(k * 128, (k + 1) * 128)
                e = jnp.exp2(s[:, lanes] * SCALE2 - m)
                e_v[j, rows, lanes] = e
                t = t + e
                d = d + e * dp[:, lanes]
            tot[rows, :] = t
            dsum[rows, :] = d
        for copy in outgoing(j):
            copy.start()
        return 0

    lax.fori_loop(0, NBLK, weigh, 0)
    near = lane[:, :128]
    for h, rows in enumerate(heads):
        t = jnp.sum(tot[rows, :], axis=1, keepdims=True)
        d = jnp.sum(dsum[rows, :], axis=1, keepdims=True)
        x = jnp.where(near == 0, top[rows, :], jnp.where(near == 1, t, d)).T
        for k in range(3):
            line = x[k : k + 1, :]
            for peer in range(PEERS):
                stat[peer, k * 8 + h : k * 8 + h + 1, :] = line
    for j in range(NBLK):
        for copy in outgoing(j):
            copy.wait()
    for copy in saves:
        copy.wait()


def run_pass_one(base, offsets, qt, wuk, wuv, og, lat_t):
    big = (NBLK, ALL, BLK)
    outs = [(big, f32), (big, f32), ((ALL, WIDE), bf16), ((ALL, LAT), bf16)]
    outs += [((PEERS, 24, 128), f32)]
    column = pltpu.VMEM((ALL, 128), f32)
    return pl.pallas_call(
        pass_one,
        in_specs=[in_smem, in_vmem] + [in_hbm] * 5,
        out_specs=[in_hbm] * 4 + [in_vmem],
        out_shape=[jax.ShapeDtypeStruct(shape, kind) for shape, kind in outs],
        scratch_shapes=[pltpu.VMEM(a.shape, bf16) for a in (qt, wuk, wuv, og, lat_t)]
        + [
            column,
            pltpu.VMEM((ALL, WIDE), bf16),
            pltpu.VMEM((ALL, LAT), bf16),
            pltpu.VMEM(big, f32),
            pltpu.VMEM(big, f32),
            column,
            column,
            column,
            pltpu.VMEM((ROWS, BLK), f32),
            pltpu.SemaphoreType.DMA((5,)),
            pltpu.SemaphoreType.DMA((NBLK,)),
            pltpu.SemaphoreType.DMA((NBLK,)),
            pltpu.SemaphoreType.DMA((2,)),
        ],
        compiler_params=params(60 * 1024 * 1024),
        name="pass_one",
    )(base, offsets, qt, wuk, wuv, og, lat_t)


def turn(qcat, dlat, qcat_t, dlat_t):
    for h in range(HEADS):
        rows = slice(h * ROWS, (h + 1) * ROWS)
        for k in range(LAT // 128):
            lanes = slice(k * 128, (k + 1) * 128)
            qcat_t[lanes, rows] = qcat[rows, lanes].T
            dlat_t[lanes, rows] = dlat[rows, lanes].T
        qcat_t[LAT:, rows] = qcat[rows, LAT:].T


def run_turn(qcat, dlat):
    return call(turn, "turn", [((WIDE, ALL), bf16), ((LAT, ALL), bf16)], (qcat, dlat))


def place(half, r):
    return jnp.where(half == 0, r[0] * 4 + r[1] * 2 + r[2], r[1] * 4 + r[2] * 2 + r[0])


def key_block(r0, r1, sc):
    return sc[3] * 4 + jnp.bitwise_xor(sc[1], r1) * 2 + jnp.bitwise_xor(sc[0], r0)


def second_load(sc, e, dp, e_v, dp_v, sem):
    loads = []
    for i in range(4):
        kb = key_block(i & 1, i >> 1, sc)
        loads.append(
            (
                pltpu.make_async_copy(e.at[kb], e_v.at[i], sem.at[0, i]),
                pltpu.make_async_copy(dp.at[kb], dp_v.at[i], sem.at[1, i]),
            )
        )
        for copy in loads[i]:
            copy.start()
    return loads


def second_core(sc, loads, qcat_t, dlat_t, coef, delta, x_out, ds_out, e_v, dp_v, pb):
    for i in range(4):
        for copy in loads[i]:
            copy.wait()
        for c in range(ALL // CHUNK):
            rows = slice(c * CHUNK, (c + 1) * CHUNK)
            cf, dl = coef[rows, :], delta[rows, :]
            for k in range(BLK // 128):
                lanes = slice(k * 128, (k + 1) * 128)
                p = e_v[i, rows, lanes] * cf
                pb[i, rows, lanes] = p.astype(bf16)
                ds_out[i, rows, lanes] = (p * (dp_v[i, rows, lanes] - dl)).astype(bf16)
        scores = dot(qcat_t[...], ds_out[i]) * SCALE
        values = dot(dlat_t[...], pb[i])
        low = (scores[:LAT] + values).astype(bf16)
        high = scores[LAT:].astype(bf16)
        for h in range(2):
            at = place(sc[3], (i & 1, i >> 1, jnp.bitwise_xor(sc[2], h)))
            if h == 0:
                x_out[at] = low[:COLS]
            else:
                x_out[at, : LAT - COLS, :] = low[COLS:]
                x_out[at, LAT - COLS :, :] = high


def second_first(
    sc, stat, qcat_t, dlat_t, e, dp, x_out, ds_out, coef, delta, e_v, dp_v, pb, sem
):
    loads = second_load(sc, e, dp, e_v, dp_v, sem)
    m = stat[:, 0:8, :]
    best = jnp.max(m, axis=0)
    w = jnp.exp2(m - best[None])
    total = jnp.sum(w * stat[:, 8:16, :], axis=0)
    dtotal = jnp.sum(w * stat[:, 16:24, :], axis=0)
    cf = jnp.exp2(stat[sc[4], 0:8, :] - best) / total
    dl = dtotal / total
    for h in range(HEADS):
        rows = slice(h * ROWS, (h + 1) * ROWS)
        coef[rows, :] = jnp.broadcast_to(cf[h : h + 1], (128, 128)).T
        delta[rows, :] = jnp.broadcast_to(dl[h : h + 1], (128, 128)).T
    second_core(sc, loads, qcat_t, dlat_t, coef, delta, x_out, ds_out, e_v, dp_v, pb)


def second_later(
    sc, coef, delta, qcat_t, dlat_t, e, dp, x_out, ds_out, e_v, dp_v, pb, sem
):
    loads = second_load(sc, e, dp, e_v, dp_v, sem)
    second_core(sc, loads, qcat_t, dlat_t, coef, delta, x_out, ds_out, e_v, dp_v, pb)


def run_second(sc, heads_in, e, dp, qcat_t, dlat_t, first):
    outs = [((8, COLS, BLK), bf16), ((4, ALL, BLK), bf16)]
    if first:
        outs += [((ALL, 128), f32)] * 2
    return pl.pallas_call(
        second_first if first else second_later,
        in_specs=[in_smem] + [in_vmem] * (len(heads_in) + 2) + [in_hbm] * 2,
        out_specs=[in_vmem] * len(outs),
        out_shape=[jax.ShapeDtypeStruct(shape, kind) for shape, kind in outs],
        scratch_shapes=[
            pltpu.VMEM((4, ALL, BLK), f32),
            pltpu.VMEM((4, ALL, BLK), f32),
            pltpu.VMEM((4, ALL, BLK), bf16),
            pltpu.SemaphoreType.DMA((2, 4)),
        ],
        compiler_params=params(50 * 1024 * 1024),
        name="second_first" if first else "second_later",
    )(sc, *heads_in, qcat_t, dlat_t, e, dp)


def query_grad(sc_a, sc_b, ds_a, ds_b, lat, wuk, out, acc, wide):
    for n, (sc, ds) in enumerate(((sc_a, ds_a), (sc_b, ds_b))):
        for i in range(4):
            kb = key_block(i & 1, i >> 1, sc)
            part = dot_nt(ds[i], lat[:, pl.ds(pl.multiple_of(kb * BLK, BLK), BLK)])
            acc[...] = part if n + i == 0 else acc[...] + part
    for h in range(HEADS):
        rows = slice(h * ROWS, (h + 1) * ROWS)
        x = acc[rows, :LAT] * SCALE
        hi = x.astype(bf16)
        lo = (x - hi.astype(f32)).astype(bf16)
        wide[h, :, :NOPE] = dot_nt(hi, wuk[h]) + dot_nt(lo, wuk[h])
        wide[h, :, NOPE:] = acc[rows, LAT:] * SCALE
    for g in range(PEERS):
        out[g] = wide[:, g * 8 : (g + 1) * 8, :].reshape(HEADS * 8, NOPE + ROT).astype(bf16)


def run_query_grad(sc_a, sc_b, ds_a, ds_b, lat_t, wuk):
    outs = [((PEERS, HEADS * 8, NOPE + ROT), bf16)]
    scratch = [pltpu.VMEM((ALL, WIDE), f32), pltpu.VMEM((HEADS, ROWS, NOPE + ROT), f32)]
    args = (sc_a, sc_b, ds_a, ds_b, lat_t, wuk)
    return call(query_grad, "query_grad", outs, args, 2, scratch)[0]


def halve(kept, got, *outs):
    n = kept.shape[0]
    for k in range(n):
        total = (kept[k].astype(f32) + got[k].astype(f32)).astype(bf16)
        outs[k * len(outs) // n][k % (n // len(outs))] = total


def run_halve(kept, got):
    n = kept.shape[0]
    outs = [((max(n // 2, 1), COLS, BLK), bf16)] * min(n, 2)
    return call(halve, "halve", outs, (kept, got))


def join(own, got, out):
    n = own.shape[0]
    out[:n] = own[...]
    out[n:] = got[...]


def run_join(own, got):
    return call(join, "join", [((2 * own.shape[0], COLS, BLK), bf16)], (own, got))[0]


def settle(sc, mine, mine_far, other, other_far, out):
    for near, far, half in ((mine, mine_far, sc[3]), (other, other_far, 1 - sc[3])):
        for i in range(8):
            b = (i >> 2 & 1, i >> 1 & 1, i & 1)
            r = [jnp.where(half == 0, b[d], b[(d + 2) % 3]) for d in range(3)]
            a = [jnp.bitwise_xor(sc[d], r[d]) for d in range(3)]
            rows = pl.ds(pl.multiple_of(a[2] * COLS, 32), COLS)
            lanes = pl.ds(pl.multiple_of((half * 4 + a[1] * 2 + a[0]) * BLK, BLK), BLK)
            out[rows, lanes] = near[i] if i < 4 else far[i - 4]


def run_settle(sc, *pieces):
    return call(settle, "settle", [((WIDE, KEYS), bf16)], (sc, *pieces), 1)[0]


def cube_neighbour(k, d):
    y, rest = k >> 2, k & 3
    if d == 2:
        return k ^ 2
    gray = (y ^ (y >> 1)) ^ (1 << d)
    back = gray ^ (gray >> 1)
    return back * 4 + rest


def along(value, n):
    pairs = [(k, cube_neighbour(k, (n + (k & 1)) % 3)) for k in range(16)]
    return lax.ppermute(value, "head", pairs)


def to_sibling(value):
    return lax.ppermute(value, "head", [(k, k ^ 1) for k in range(16)])


def shards(queries, w_uk, w_uv, latent, out_grad, offsets):
    head = lax.axis_index("head").astype(jnp.int32)
    key = lax.axis_index("key").astype(jnp.int32)
    y = head >> 2
    gray = y ^ (y >> 1)
    core = head & 1
    sc_own = jnp.stack([gray & 1, gray >> 1, (head >> 1) & 1, core, key])
    sc_far = jnp.stack([gray & 1, gray >> 1, (head >> 1) & 1, 1 - core, key])
    lat_t = latent.T
    qt = jnp.transpose(queries, (1, 2, 0))
    og = out_grad.reshape(ALL, 128)
    e, dp, qcat, dlat, stat = run_pass_one(
        (key * KEYS)[None], offsets[None], qt, w_uk, w_uv, og, lat_t
    )
    stat = lax.all_to_all(stat, "key", 0, 0, tiled=True)
    qcat_t, dlat_t = run_turn(qcat, dlat)
    x_far, ds_far, coef, delta = run_second(sc_far, (stat,), e, dp, qcat_t, dlat_t, True)
    came = to_sibling(x_far)
    x_own, ds_own = run_second(sc_own, (coef, delta), e, dp, qcat_t, dlat_t, False)
    kept, send = run_halve(x_own, came)
    got = along(send, 0)
    dq = run_query_grad(sc_far, sc_own, ds_far, ds_own, lat_t, w_uk)
    got, dq = lax.optimization_barrier((got, dq))
    kept, send = run_halve(kept, got)
    send, dq = lax.optimization_barrier((send, dq))
    got = along(send, 1)
    dq = lax.all_to_all(dq, "key", 0, 0, tiled=True)
    kept, send = run_halve(kept, got)
    (own,) = run_halve(kept, along(send, 2))
    own = run_join(own, along(own, 2))
    own, dq = lax.optimization_barrier((own, dq))
    near = run_join(own, along(own, 1))
    far = along(near, 0)
    d_latent = run_settle(sc_own, near, far, to_sibling(near), to_sibling(far)).T

    total = jnp.sum(dq.astype(f32), axis=0).astype(bf16)
    d_queries = jnp.transpose(total.reshape(HEADS, 8, NOPE + ROT), (1, 0, 2))
    return (d_queries, d_latent)


def solution(mesh):
    return jax.shard_map(
        shards,
        mesh=mesh,
        in_specs=(
            P(None, "head", None),
            P("head", None, None),
            P("head", None, None),
            P("key", None),
            P(None, "head", None),
            P(),
        ),
        out_specs=(P("key", "head", None), P("key", None)),
        check_vma=False,
    )
```

```python
import functools
import math

import jax
import jax.numpy as jnp
from jax import lax
from jax.experimental import pallas as pl
from jax.experimental.pallas import tpu as pltpu
from jax.sharding import PartitionSpec as P

bf16 = jnp.bfloat16
f32 = jnp.float32
floor_score = -1e30
floor_top = -1e20

HEADS = 8
ROWS = 128
NOPE = 128
ROT = 64
LAT = 512
WIDE = LAT + ROT
KEYS = 2048
BLK = 256
NBLK = KEYS // BLK
ALL = HEADS * ROWS
PEERS = 16
COLS = WIDE // 4
CHAINS = 2
SCALE = 1.0 / math.sqrt(NOPE + ROT)
SCALE2 = SCALE * math.log2(math.e)
VLIM = 12 * 1024 * 1024

NT = (((1,), (1,)), ((), ()))


def dot(a, b):
    return jnp.dot(a, b, preferred_element_type=f32)


def dot_nt(a, b):
    return lax.dot_general(a, b, NT, preferred_element_type=f32)


def params(limit=VLIM):
    return pltpu.CompilerParams(vmem_limit_bytes=limit)


in_vmem = pl.BlockSpec(memory_space=pltpu.VMEM)
in_hbm = pl.BlockSpec(memory_space=pltpu.HBM)
in_smem = pl.BlockSpec(memory_space=pltpu.SMEM)


def call(kernel, name, outs, args, scalars=0, scratch=(), limit=VLIM):
    return pl.pallas_call(
        kernel,
        in_specs=[in_smem] * scalars + [in_vmem] * (len(args) - scalars),
        out_specs=[in_vmem] * len(outs),
        out_shape=[jax.ShapeDtypeStruct(shape, kind) for shape, kind in outs],
        scratch_shapes=list(scratch),
        compiler_params=params(limit),
        name=name,
    )(*args)


CHUNK = 256


def pass_one(
    base, off, qt, wuk, wuv, og, lat,
    e_v, dp_v, qcat_t, dlat_t, stat,
    qt_v, wuk_v, wuv_v, og_v, lat_v, og_wide, qcat, dlat, top, tot, dsum, hide, sem_in,
):
    pairs = ((qt, qt_v), (wuk, wuk_v), (og, og_v), (wuv, wuv_v), (lat, lat_v))
    loads = [pltpu.make_async_copy(a, b, sem_in.at[k]) for k, (a, b) in enumerate(pairs)]
    for copy in loads:
        copy.start()
    bound = jnp.broadcast_to(off[...], (ROWS, ROWS)).T - base[0]
    bound = jnp.concatenate([bound] * (BLK // 128), axis=1)
    lane = lax.broadcasted_iota(jnp.int32, (ROWS, BLK), 1)
    top[...] = jnp.full((ALL, 128), floor_top, f32)
    tot[...] = jnp.zeros((ALL, 128), f32)
    dsum[...] = jnp.zeros((ALL, 128), f32)
    chunks = [slice(c * CHUNK, (c + 1) * CHUNK) for c in range(ALL // CHUNK)]
    heads = [slice(h * ROWS, (h + 1) * ROWS) for h in range(HEADS)]

    loads[0].wait()
    loads[1].wait()
    for h, rows in enumerate(heads):
        q = qt_v[h].T
        qcat[rows, :LAT] = dot(q[:, :NOPE], wuk_v[h]).astype(bf16)
        qcat[rows, LAT:] = q[:, NOPE:]
    loads[2].wait()
    loads[3].wait()
    og_wide[...] = og_v[...].astype(f32)
    for h, rows in enumerate(heads):
        grad = og_wide[pl.ds(h, ROWS, stride=HEADS), :].astype(bf16)
        dlat[rows, :] = dot_nt(grad, wuv_v[h]).astype(bf16)
    loads[4].wait()
    for rows in heads:
        for k in range(LAT // 128):
            lanes = slice(k * 128, (k + 1) * 128)
            qcat_t[lanes, rows] = qcat[rows, lanes].T
            dlat_t[lanes, rows] = dlat[rows, lanes].T
        qcat_t[LAT:, rows] = qcat[rows, LAT:].T

    def score(j, _):
        at = pl.multiple_of(j * BLK, BLK)
        hide[...] = jnp.where(lane + at <= bound, 0.0, floor_score)
        cols = lat_v[:, pl.ds(at, BLK)]
        for rows in chunks:
            s = dot(qcat[rows, :], cols)
            s = (s.reshape(CHUNK // ROWS, ROWS, BLK) + hide[...][None]).reshape(CHUNK, BLK)
            e_v[j, rows, :] = s
            best = top[rows, :]
            for k in range(BLK // 128):
                best = jnp.maximum(best, s[:, k * 128 : (k + 1) * 128])
            top[rows, :] = best
        return 0

    lax.fori_loop(0, NBLK, score, 0)
    top[...] = jnp.broadcast_to(jnp.max(top[...], axis=1, keepdims=True) * SCALE2, (ALL, 128))

    def weigh(j, _):
        cols = lat_v[:LAT, pl.ds(pl.multiple_of(j * BLK, BLK), BLK)]
        for rows in chunks:
            dp = dot(dlat[rows, :], cols)
            dp_v[j, rows, :] = dp
            s = e_v[j, rows, :]
            m = top[rows, :]
            t, d = tot[rows, :], dsum[rows, :]
            for k in range(BLK // 128):
                lanes = slice(k * 128, (k + 1) * 128)
                e = jnp.exp2(s[:, lanes] * SCALE2 - m)
                e_v[j, rows, lanes] = e
                t = t + e
                d = d + e * dp[:, lanes]
            tot[rows, :] = t
            dsum[rows, :] = d
        return 0

    lax.fori_loop(0, NBLK, weigh, 0)
    near = lane[:, :128]
    for h, rows in enumerate(heads):
        t = jnp.sum(tot[rows, :], axis=1, keepdims=True)
        d = jnp.sum(dsum[rows, :], axis=1, keepdims=True)
        x = jnp.where(near == 0, top[rows, :], jnp.where(near == 1, t, d)).T
        for k in range(3):
            line = x[k : k + 1, :]
            for peer in range(PEERS):
                stat[peer, k * 8 + h : k * 8 + h + 1, :] = line


def run_pass_one(base, offsets, qt, wuk, wuv, og, lat_t):
    big = (NBLK, ALL, BLK)
    outs = [(big, f32), (big, f32), ((WIDE, ALL), bf16), ((LAT, ALL), bf16)]
    outs += [((PEERS, 24, 128), f32)]
    column = pltpu.VMEM((ALL, 128), f32)
    return pl.pallas_call(
        pass_one,
        in_specs=[in_smem, in_vmem] + [in_hbm] * 5,
        out_specs=[in_vmem] * 5,
        out_shape=[jax.ShapeDtypeStruct(shape, kind) for shape, kind in outs],
        scratch_shapes=[pltpu.VMEM(a.shape, bf16) for a in (qt, wuk, wuv, og, lat_t)]
        + [
            column,
            pltpu.VMEM((ALL, WIDE), bf16),
            pltpu.VMEM((ALL, LAT), bf16),
            column,
            column,
            column,
            pltpu.VMEM((ROWS, BLK), f32),
            pltpu.SemaphoreType.DMA((5,)),
        ],
        compiler_params=params(18 * 1024 * 1024),
        name="pass_one",
    )(base, offsets, qt, wuk, wuv, og, lat_t)


def place(half, r):
    return jnp.where(half == 0, r[0] * 4 + r[1] * 2 + r[2], r[1] * 4 + r[2] * 2 + r[0])


def key_block(r0, chain, sc):
    return sc[3] * 4 + chain * 2 + jnp.bitwise_xor(sc[0], r0)


def second(chain, sc, coef, delta, qcat_t, dlat_t, e, dp, x_out, ds_out, pb):
    for i in range(2):
        kb = key_block(i, chain, sc)
        for c in range(ALL // CHUNK):
            rows = slice(c * CHUNK, (c + 1) * CHUNK)
            cf, dl = coef[rows, :], delta[rows, :]
            for k in range(BLK // 128):
                lanes = slice(k * 128, (k + 1) * 128)
                p = e[kb, rows, lanes] * cf
                pb[i, rows, lanes] = p.astype(bf16)
                ds_out[i, rows, lanes] = (p * (dp[kb, rows, lanes] - dl)).astype(bf16)
        scores = dot(qcat_t[...], ds_out[i]) * SCALE
        values = dot(dlat_t[...], pb[i])
        low = (scores[:LAT] + values).astype(bf16)
        high = scores[LAT:].astype(bf16)
        for q in range(4):
            r = (i, jnp.bitwise_xor(sc[1], q & 1), jnp.bitwise_xor(sc[2], q >> 1))
            at = place(sc[3], r)
            if q < 3:
                x_out[at] = low[q * COLS : (q + 1) * COLS]
            else:
                x_out[at, : LAT - 3 * COLS, :] = low[3 * COLS :]
                x_out[at, LAT - 3 * COLS :, :] = high


def second_first(sc, stat, qcat_t, dlat_t, e, dp, x_out, ds_out, coef, delta, pb):
    m = stat[:, 0:8, :]
    best = jnp.max(m, axis=0)
    w = jnp.exp2(m - best[None])
    total = jnp.sum(w * stat[:, 8:16, :], axis=0)
    dtotal = jnp.sum(w * stat[:, 16:24, :], axis=0)
    cf = jnp.exp2(stat[sc[4], 0:8, :] - best) / total
    dl = dtotal / total
    for h in range(HEADS):
        rows = slice(h * ROWS, (h + 1) * ROWS)
        coef[rows, :] = jnp.broadcast_to(cf[h : h + 1], (128, 128)).T
        delta[rows, :] = jnp.broadcast_to(dl[h : h + 1], (128, 128)).T
    second(0, sc, coef, delta, qcat_t, dlat_t, e, dp, x_out, ds_out, pb)


def run_second(sc, heads_in, qcat_t, dlat_t, e, dp, chain):
    first = len(heads_in) == 1
    outs = [((8, COLS, BLK), bf16), ((2, ALL, BLK), bf16)]
    if first:
        outs += [((ALL, 128), f32)] * 2
    return call(
        second_first if first else functools.partial(second, chain),
        "second_first" if first else "second",
        outs,
        (sc, *heads_in, qcat_t, dlat_t, e, dp),
        1,
        [pltpu.VMEM((2, ALL, BLK), bf16)],
    )


def query_grad(sc_far, sc_own, far_a, own_a, far_b, own_b, lat, wuk, out, acc, wide):
    first = True
    for chain, half_ds in enumerate(((far_a, own_a), (far_b, own_b))):
        for sc, ds in zip((sc_far, sc_own), half_ds):
            for i in range(2):
                kb = key_block(i, chain, sc)
                part = dot_nt(ds[i], lat[:, pl.ds(pl.multiple_of(kb * BLK, BLK), BLK)])
                acc[...] = part if first else acc[...] + part
                first = False
    for h in range(HEADS):
        rows = slice(h * ROWS, (h + 1) * ROWS)
        x = acc[rows, :LAT] * SCALE
        hi = x.astype(bf16)
        lo = (x - hi.astype(f32)).astype(bf16)
        wide[h, :, :NOPE] = dot_nt(hi, wuk[h]) + dot_nt(lo, wuk[h])
        wide[h, :, NOPE:] = acc[rows, LAT:] * SCALE
    for g in range(PEERS):
        out[g] = wide[:, g * 8 : (g + 1) * 8, :].reshape(HEADS * 8, NOPE + ROT).astype(bf16)


def run_query_grad(*args):
    outs = [((PEERS, HEADS * 8, NOPE + ROT), bf16)]
    scratch = [pltpu.VMEM((ALL, WIDE), f32), pltpu.VMEM((HEADS, ROWS, NOPE + ROT), f32)]
    return call(query_grad, "query_grad", outs, args, 2, scratch)[0]


def halve(kept, got, *outs):
    n = kept.shape[0]
    for k in range(n):
        total = (kept[k].astype(f32) + got[k].astype(f32)).astype(bf16)
        outs[k * len(outs) // n][k % (n // len(outs))] = total


def run_halve(kept, got):
    n = kept.shape[0]
    outs = [((max(n // 2, 1), COLS, BLK), bf16)] * min(n, 2)
    return call(halve, "halve", outs, (kept, got))


def join(own, got, out):
    n = own.shape[0]
    out[:n] = own[...]
    out[n:] = got[...]


def run_join(own, got):
    return call(join, "join", [((2 * own.shape[0], COLS, BLK), bf16)], (own, got))[0]


def settle(sc, *refs):
    out = refs[-1]
    for chain in range(CHAINS):
        mine, mine_far, other, other_far = refs[4 * chain : 4 * chain + 4]
        for near, far, half in ((mine, mine_far, sc[3]), (other, other_far, 1 - sc[3])):
            for i in range(8):
                b = (i >> 2 & 1, i >> 1 & 1, i & 1)
                r = [jnp.where(half == 0, b[d], b[(d + 2) % 3]) for d in range(3)]
                a = [jnp.bitwise_xor(sc[d], r[d]) for d in range(3)]
                rows = pl.ds(pl.multiple_of((a[2] * 2 + a[1]) * COLS, 16), COLS)
                block = half * 4 + chain * 2 + a[0]
                lanes = pl.ds(pl.multiple_of(block * BLK, BLK), BLK)
                out[rows, lanes] = near[i] if i < 4 else far[i - 4]


def run_settle(sc, *pieces):
    return call(settle, "settle", [((WIDE, KEYS), bf16)], (sc, *pieces), 1)[0]


def cube_neighbour(k, d):
    y, rest = k >> 2, k & 3
    if d == 2:
        return k ^ 2
    gray = (y ^ (y >> 1)) ^ (1 << d)
    back = gray ^ (gray >> 1)
    return back * 4 + rest


def along(value, n):
    pairs = [(k, cube_neighbour(k, (n + (k & 1)) % 3)) for k in range(16)]
    return lax.ppermute(value, "head", pairs)


def to_sibling(value):
    return lax.ppermute(value, "head", [(k, k ^ 1) for k in range(16)])


def held(value):
    return pltpu.with_memory_space_constraint(value, pltpu.HBM)


def shards(queries, w_uk, w_uv, latent, out_grad, offsets):
    head = lax.axis_index("head").astype(jnp.int32)
    key = lax.axis_index("key").astype(jnp.int32)
    y = head >> 2
    gray = y ^ (y >> 1)
    core = head & 1
    sc_own = jnp.stack([gray & 1, gray >> 1, (head >> 1) & 1, core, key])
    sc_far = jnp.stack([gray & 1, gray >> 1, (head >> 1) & 1, 1 - core, key])
    lat_t = latent.T
    qt = jnp.transpose(queries, (1, 2, 0))
    og = out_grad.reshape(ALL, 128)
    e, dp, qcat_t, dlat_t, stat = run_pass_one(
        (key * KEYS)[None], offsets[None], *map(held, (qt, w_uk, w_uv, og, lat_t))
    )
    stat, sc_own, sc_far = lax.optimization_barrier((stat, sc_own, sc_far))
    stat = lax.all_to_all(stat, "key", 0, 0, tiled=True)
    turned = (qcat_t, dlat_t, e, dp)
    x_far, far_a, coef, delta = run_second(sc_far, (stat,), *turned, 0)
    came = to_sibling(x_far)
    x_own, own_a = run_second(sc_own, (coef, delta), *turned, 0)
    kept_a, send_a = run_halve(x_own, came)
    tie = lax.optimization_barrier
    sc_late, send_a = tie((sc_far, send_a))
    got_a = along(send_a, 0)
    x_far, far_b = run_second(sc_late, (coef, delta), *turned, 1)
    came = to_sibling(x_far)
    x_own, own_b = run_second(sc_own, (coef, delta), *turned, 1)
    kept_b, send_b = run_halve(x_own, came)
    got_b = along(send_b, 0)
    dq = run_query_grad(sc_far, sc_own, far_a, own_a, far_b, own_b, lat_t, w_uk)
    got_a, dq = tie((got_a, dq))
    kept_a, send_a = run_halve(kept_a, got_a)
    kept_b, send_a, dq = tie((kept_b, send_a, dq))
    got_a = along(send_a, 1)
    dq = lax.all_to_all(dq, "key", 0, 0, tiled=True)
    kept_b, send_b = run_halve(kept_b, got_b)
    kept_a, send_b = tie((kept_a, send_b))
    got_b = along(send_b, 1)
    kept_a, send_a = run_halve(kept_a, got_a)
    kept_b, send_a = tie((kept_b, send_a))
    got_a = along(send_a, 2)
    kept_b, send_b = run_halve(kept_b, got_b)
    kept_a, send_b = tie((kept_a, send_b))
    got_b = along(send_b, 2)
    (own_a,) = run_halve(kept_a, got_a)
    kept_b, own_a = tie((kept_b, own_a))
    got_a = along(own_a, 2)
    (own_b,) = run_halve(kept_b, got_b)
    own_a, own_b = tie((own_a, own_b))
    got_b = along(own_b, 2)
    own_a = run_join(own_a, got_a)
    own_b, own_a = tie((own_b, own_a))
    got_a = along(own_a, 1)
    own_b = run_join(own_b, got_b)
    own_a, own_b, dq = tie((own_a, own_b, dq))
    got_b = along(own_b, 1)
    own_a = run_join(own_a, got_a)
    own_b, own_a = tie((own_b, own_a))
    far_a, near_a = along(own_a, 0), to_sibling(own_a)
    own_b = run_join(own_b, got_b)
    far_b, near_b = along(own_b, 0), to_sibling(own_b)
    pieces = [
        (own_a, far_a, near_a, to_sibling(far_a)),
        (own_b, far_b, near_b, to_sibling(far_b)),
    ]
    d_latent = run_settle(sc_own, *pieces[0], *pieces[1]).T

    total = jnp.sum(dq.astype(f32), axis=0).astype(bf16)
    d_queries = jnp.transpose(total.reshape(HEADS, 8, NOPE + ROT), (1, 0, 2))
    return (d_queries, d_latent)


def solution(mesh):
    return jax.shard_map(
        shards,
        mesh=mesh,
        in_specs=(
            P(None, "head", None),
            P("head", None, None),
            P("head", None, None),
            P("key", None),
            P(None, "head", None),
            P(),
        ),
        out_specs=(P("key", "head", None), P("key", None)),
        check_vma=False,
    )
```

```python
import functools
import math

import jax
import jax.numpy as jnp
from jax import lax
from jax.experimental import pallas as pl
from jax.experimental.pallas import tpu as pltpu
from jax.sharding import PartitionSpec as P

bf16 = jnp.bfloat16
f32 = jnp.float32
floor_score = -1e30
floor_top = -1e20

HEADS = 8
ROWS = 128
NOPE = 128
ROT = 64
LAT = 512
WIDE = LAT + ROT
KEYS = 2048
BLK = 256
NBLK = KEYS // BLK
ALL = HEADS * ROWS
PEERS = 16
COLS = WIDE // 4
CHAINS = 2
SCALE = 1.0 / math.sqrt(NOPE + ROT)
SCALE2 = SCALE * math.log2(math.e)
VLIM = 14 * 1024 * 1024
LIMIT_ONE = 34 * 1024 * 1024
LIMIT_TWO = 28 * 1024 * 1024

NT = (((1,), (1,)), ((), ()))


def dot(a, b):
    return jnp.dot(a, b, preferred_element_type=f32)


def dot_nt(a, b):
    return lax.dot_general(a, b, NT, preferred_element_type=f32)


def params(limit=VLIM):
    return pltpu.CompilerParams(vmem_limit_bytes=limit)


in_vmem = pl.BlockSpec(memory_space=pltpu.VMEM)
in_hbm = pl.BlockSpec(memory_space=pltpu.HBM)
in_smem = pl.BlockSpec(memory_space=pltpu.SMEM)


def call(kernel, name, outs, args, scalars=0, scratch=(), limit=VLIM):
    return pl.pallas_call(
        kernel,
        in_specs=[in_smem] * scalars + [in_vmem] * (len(args) - scalars),
        out_specs=[in_vmem] * len(outs),
        out_shape=[jax.ShapeDtypeStruct(shape, kind) for shape, kind in outs],
        scratch_shapes=list(scratch),
        compiler_params=params(limit),
        name=name,
    )(*args)


CHUNK = 256


def pass_one(
    base, off, qt, wuk, wuv, og, lat,
    e_v, dp_v, qcat_t, dlat_t, stat,
    off_v, qt_v, wuk_v, wuv_v, og_v, lat_v, og_wide, qcat, dlat, top, tot, dsum, hide, sem_in,
):
    pairs = ((off, off_v), (qt, qt_v), (wuk, wuk_v), (og, og_v), (wuv, wuv_v), (lat, lat_v))
    loads = [pltpu.make_async_copy(a, b, sem_in.at[k]) for k, (a, b) in enumerate(pairs)]
    for copy in loads:
        copy.start()
    loads[0].wait()
    bound = jnp.broadcast_to(off_v[...], (ROWS, ROWS)).T - base[0]
    bound = jnp.concatenate([bound] * (BLK // 128), axis=1)
    lane = lax.broadcasted_iota(jnp.int32, (ROWS, BLK), 1)
    top[...] = jnp.full((ALL, 128), floor_top, f32)
    tot[...] = jnp.zeros((ALL, 128), f32)
    dsum[...] = jnp.zeros((ALL, 128), f32)
    chunks = [slice(c * CHUNK, (c + 1) * CHUNK) for c in range(ALL // CHUNK)]
    heads = [slice(h * ROWS, (h + 1) * ROWS) for h in range(HEADS)]

    loads[1].wait()
    loads[2].wait()
    for h, rows in enumerate(heads):
        q = qt_v[h].T
        qcat[rows, :LAT] = dot(q[:, :NOPE], wuk_v[h]).astype(bf16)
        qcat[rows, LAT:] = q[:, NOPE:]
    loads[3].wait()
    loads[4].wait()
    og_wide[...] = og_v[...].astype(f32)
    for h, rows in enumerate(heads):
        grad = og_wide[pl.ds(h, ROWS, stride=HEADS), :].astype(bf16)
        dlat[rows, :] = dot_nt(grad, wuv_v[h]).astype(bf16)
    loads[5].wait()
    for rows in heads:
        for k in range(LAT // 128):
            lanes = slice(k * 128, (k + 1) * 128)
            qcat_t[lanes, rows] = qcat[rows, lanes].T
            dlat_t[lanes, rows] = dlat[rows, lanes].T
        qcat_t[LAT:, rows] = qcat[rows, LAT:].T

    def score(j, _):
        at = pl.multiple_of(j * BLK, BLK)
        hide[...] = jnp.where(lane + at <= bound, 0.0, floor_score)
        cols = lat_v[:, pl.ds(at, BLK)]
        for rows in chunks:
            s = dot(qcat[rows, :], cols)
            s = (s.reshape(CHUNK // ROWS, ROWS, BLK) + hide[...][None]).reshape(CHUNK, BLK)
            e_v[j, rows, :] = s
            best = top[rows, :]
            for k in range(BLK // 128):
                best = jnp.maximum(best, s[:, k * 128 : (k + 1) * 128])
            top[rows, :] = best
        return 0

    lax.fori_loop(0, NBLK, score, 0)
    top[...] = jnp.broadcast_to(jnp.max(top[...], axis=1, keepdims=True) * SCALE2, (ALL, 128))

    def weigh(j, _):
        cols = lat_v[:LAT, pl.ds(pl.multiple_of(j * BLK, BLK), BLK)]
        for rows in chunks:
            dp = dot(dlat[rows, :], cols)
            dp_v[j, rows, :] = dp
            s = e_v[j, rows, :]
            m = top[rows, :]
            t, d = tot[rows, :], dsum[rows, :]
            for k in range(BLK // 128):
                lanes = slice(k * 128, (k + 1) * 128)
                e = jnp.exp2(s[:, lanes] * SCALE2 - m)
                e_v[j, rows, lanes] = e
                t = t + e
                d = d + e * dp[:, lanes]
            tot[rows, :] = t
            dsum[rows, :] = d
        return 0

    lax.fori_loop(0, NBLK, weigh, 0)
    near = lane[:, :128]
    for h, rows in enumerate(heads):
        t = jnp.sum(tot[rows, :], axis=1, keepdims=True)
        d = jnp.sum(dsum[rows, :], axis=1, keepdims=True)
        x = jnp.where(near == 0, top[rows, :], jnp.where(near == 1, t, d)).T
        for k in range(3):
            line = x[k : k + 1, :]
            for peer in range(PEERS):
                stat[peer, k * 8 + h : k * 8 + h + 1, :] = line


def run_pass_one(base, offsets, qt, wuk, wuv, og, lat_t):
    big = (NBLK, ALL, BLK)
    outs = [(big, f32), (big, f32), ((WIDE, ALL), bf16), ((LAT, ALL), bf16)]
    outs += [((PEERS, 24, 128), f32)]
    column = pltpu.VMEM((ALL, 128), f32)
    return pl.pallas_call(
        pass_one,
        in_specs=[in_smem] + [in_hbm] * 6,
        out_specs=[in_vmem] * 5,
        out_shape=[jax.ShapeDtypeStruct(shape, kind) for shape, kind in outs],
        scratch_shapes=[pltpu.VMEM(a.shape, a.dtype) for a in (offsets, qt, wuk, wuv, og, lat_t)]
        + [
            column,
            pltpu.VMEM((ALL, WIDE), bf16),
            pltpu.VMEM((ALL, LAT), bf16),
            column,
            column,
            column,
            pltpu.VMEM((ROWS, BLK), f32),
            pltpu.SemaphoreType.DMA((6,)),
        ],
        compiler_params=params(LIMIT_ONE),
        name="pass_one",
    )(base, offsets, qt, wuk, wuv, og, lat_t)


def place(half, r):
    return jnp.where(half == 0, r[0] * 4 + r[1] * 2 + r[2], r[1] * 4 + r[2] * 2 + r[0])


def key_block(r0, chain, sc):
    return sc[3] * 4 + chain * 2 + jnp.bitwise_xor(sc[0], r0)


TALL = 512


def second(chain, sc, coef, delta, qcat_t, dlat_t, e, dp, x_out, ds_out):
    for i in range(2):
        kb = key_block(i, chain, sc)
        scores = values = None
        for c in range(ALL // TALL):
            rows = slice(c * TALL, (c + 1) * TALL)
            cf = jnp.concatenate([coef[rows, :]] * (BLK // 128), axis=1)
            dl = jnp.concatenate([delta[rows, :]] * (BLK // 128), axis=1)
            p = e[kb, rows, :] * cf
            ds = (p * (dp[kb, rows, :] - dl)).astype(bf16)
            ds_out[i, rows, :] = ds
            from_scores = dot(qcat_t[:, rows], ds)
            from_values = dot(dlat_t[:, rows], p.astype(bf16))
            scores = from_scores if c == 0 else scores + from_scores
            values = from_values if c == 0 else values + from_values
        scores = scores * SCALE
        low = (scores[:LAT] + values).astype(bf16)
        high = scores[LAT:].astype(bf16)
        for q in range(4):
            r = (i, jnp.bitwise_xor(sc[1], q & 1), jnp.bitwise_xor(sc[2], q >> 1))
            at = place(sc[3], r)
            if q < 3:
                x_out[at] = low[q * COLS : (q + 1) * COLS]
            else:
                x_out[at, : LAT - 3 * COLS, :] = low[3 * COLS :]
                x_out[at, LAT - 3 * COLS :, :] = high


def second_first(sc, stat, qcat_t, dlat_t, e, dp, x_out, ds_out, coef, delta):
    m = stat[:, 0:8, :]
    best = jnp.max(m, axis=0)
    w = jnp.exp2(m - best[None])
    total = jnp.sum(w * stat[:, 8:16, :], axis=0)
    dtotal = jnp.sum(w * stat[:, 16:24, :], axis=0)
    cf = jnp.exp2(stat[sc[4], 0:8, :] - best) / total
    dl = dtotal / total
    for h in range(HEADS):
        rows = slice(h * ROWS, (h + 1) * ROWS)
        coef[rows, :] = jnp.broadcast_to(cf[h : h + 1], (128, 128)).T
        delta[rows, :] = jnp.broadcast_to(dl[h : h + 1], (128, 128)).T
    second(0, sc, coef, delta, qcat_t, dlat_t, e, dp, x_out, ds_out)


def run_second(sc, heads_in, qcat_t, dlat_t, e, dp, chain):
    first = len(heads_in) == 1
    outs = [((8, COLS, BLK), bf16), ((2, ALL, BLK), bf16)]
    if first:
        outs += [((ALL, 128), f32)] * 2
    return call(
        second_first if first else functools.partial(second, chain),
        "second_first" if first else "second",
        outs,
        (sc, *heads_in, qcat_t, dlat_t, e, dp),
        1,
        limit=LIMIT_TWO,
    )


def query_piece(chain, sc, ds, lat, *refs):
    total = None if len(refs) == 1 else refs[0][...]
    for i in range(2):
        kb = key_block(i, chain, sc)
        part = dot_nt(ds[i], lat[:, pl.ds(pl.multiple_of(kb * BLK, BLK), BLK)])
        total = part if total is None else total + part
    refs[-1][...] = total


def run_query_piece(chain, sc, ds, lat_t, *acc):
    kernel = functools.partial(query_piece, chain)
    return call(kernel, "query_piece", [((ALL, WIDE), f32)], (sc, ds, lat_t, *acc), 1)[0]


def query_last(sc, acc, wuk, keep, send, wide):
    for h in range(HEADS):
        rows = slice(h * ROWS, (h + 1) * ROWS)
        x = acc[rows, :LAT] * SCALE
        hi = x.astype(bf16)
        lo = (x - hi.astype(f32)).astype(bf16)
        wide[h, :, :NOPE] = dot_nt(hi, wuk[h]) + dot_nt(lo, wuk[h])
        wide[h, :, NOPE:] = acc[rows, LAT:] * SCALE
    for g in range(PEERS):
        bits = (g >> 3 & 1) | (g >> 2 & 1) << 1 | (g >> 1 & 1) << 2 | (g & 1) << 3
        owner = jnp.bitwise_xor(sc[4], bits)
        mine = wide[:, pl.ds(pl.multiple_of(owner * 8, 8), 8), :]
        half = keep if g < 8 else send
        half[g % 8] = mine.reshape(HEADS * 8, NOPE + ROT).astype(bf16)


def run_query_last(sc, acc, wuk):
    outs = [((8, HEADS * 8, NOPE + ROT), bf16)] * 2
    scratch = [pltpu.VMEM((HEADS, ROWS, NOPE + ROT), f32)]
    return call(query_last, "query_last", outs, (sc, acc, wuk), 1, scratch)


def halve(kept, got, *outs):
    n = kept.shape[0]
    for k in range(n):
        total = (kept[k].astype(f32) + got[k].astype(f32)).astype(bf16)
        outs[k * len(outs) // n][k % (n // len(outs))] = total


def run_halve(kept, got):
    n = kept.shape[0]
    outs = [((max(n // 2, 1), *kept.shape[1:]), bf16)] * min(n, 2)
    return call(halve, "halve", outs, (kept, got))


def join(own, got, out):
    n = own.shape[0]
    out[:n] = own[...]
    out[n:] = got[...]


def run_join(own, got):
    return call(join, "join", [((2 * own.shape[0], COLS, BLK), bf16)], (own, got))[0]


def settle(sc, *refs):
    out, sem = refs[-2:]
    copies = []
    for chain in range(CHAINS):
        mine, mine_far, other, other_far = refs[4 * chain : 4 * chain + 4]
        for near, far, half in ((mine, mine_far, sc[3]), (other, other_far, 1 - sc[3])):
            for i in range(8):
                b = (i >> 2 & 1, i >> 1 & 1, i & 1)
                r = [jnp.where(half == 0, b[d], b[(d + 2) % 3]) for d in range(3)]
                a = [jnp.bitwise_xor(sc[d], r[d]) for d in range(3)]
                rows = pl.ds(pl.multiple_of((a[2] * 2 + a[1]) * COLS, 16), COLS)
                block = half * 4 + chain * 2 + a[0]
                lanes = pl.ds(pl.multiple_of(block * BLK, BLK), BLK)
                block = near.at[i] if i < 4 else far.at[i - 4]
                copy = pltpu.make_async_copy(block, out.at[rows, lanes], sem.at[len(copies)])
                copy.start()
                copies.append(copy)
    for copy in copies:
        copy.wait()


def run_settle(sc, *pieces):
    return pl.pallas_call(
        settle,
        in_specs=[in_smem] + [in_vmem] * len(pieces),
        out_specs=in_hbm,
        out_shape=jax.ShapeDtypeStruct((WIDE, KEYS), bf16),
        scratch_shapes=[pltpu.SemaphoreType.DMA((16 * CHAINS,))],
        compiler_params=params(),
        name="settle",
    )(sc, *pieces)


def cube_neighbour(k, d):
    y, rest = k >> 2, k & 3
    if d == 2:
        return k ^ 2
    gray = (y ^ (y >> 1)) ^ (1 << d)
    back = gray ^ (gray >> 1)
    return back * 4 + rest


def along(value, n):
    pairs = [(k, cube_neighbour(k, (n + (k & 1)) % 3)) for k in range(16)]
    return lax.ppermute(value, "head", pairs)


def to_sibling(value):
    return lax.ppermute(value, "head", [(k, k ^ 1) for k in range(16)])


def to_key(value, flip):
    return lax.ppermute(value, "key", [(k, k ^ flip) for k in range(16)])


def held(value):
    return pltpu.with_memory_space_constraint(value, pltpu.HBM)


def shards(queries, w_uk, w_uv, latent, out_grad, offsets):
    head = lax.axis_index("head").astype(jnp.int32)
    key = lax.axis_index("key").astype(jnp.int32)
    y = head >> 2
    gray = y ^ (y >> 1)
    core = head & 1
    sc_own = jnp.stack([gray & 1, gray >> 1, (head >> 1) & 1, core, key])
    sc_far = jnp.stack([gray & 1, gray >> 1, (head >> 1) & 1, 1 - core, key])
    lat_t = latent.T
    qt = jnp.transpose(queries, (1, 2, 0))
    og = out_grad.reshape(ALL, 128)
    e, dp, qcat_t, dlat_t, stat = run_pass_one(
        (key * KEYS)[None], *map(held, (offsets[None], qt, w_uk, w_uv, og, lat_t))
    )
    stat, sc_own, sc_far = lax.optimization_barrier((stat, sc_own, sc_far))
    stat = lax.all_to_all(stat, "key", 0, 0, tiled=True)
    turned = (qcat_t, dlat_t, e, dp)
    x_far, far_a, coef, delta = run_second(sc_far, (stat,), *turned, 0)
    came = to_sibling(x_far)
    x_own, own_a = run_second(sc_own, (coef, delta), *turned, 0)
    kept_a, send_a = run_halve(x_own, came)
    tie = lax.optimization_barrier
    sc_late, send_a = tie((sc_far, send_a))
    got_a = along(send_a, 0)
    x_far, far_b = run_second(sc_late, (coef, delta), *turned, 1)
    came = to_sibling(x_far)
    x_own, own_b = run_second(sc_own, (coef, delta), *turned, 1)
    kept_b, send_b = run_halve(x_own, came)
    got_b = along(send_b, 0)
    acc = run_query_piece(0, sc_far, far_a, lat_t)
    acc = run_query_piece(0, sc_own, own_a, lat_t, acc)
    got_a, acc = tie((got_a, acc))
    kept_a, send_a = run_halve(kept_a, got_a)
    kept_b, send_a, acc = tie((kept_b, send_a, acc))
    got_a = along(send_a, 1)
    acc = run_query_piece(1, sc_far, far_b, lat_t, acc)
    acc = run_query_piece(1, sc_own, own_b, lat_t, acc)
    got_b, acc = tie((got_b, acc))
    kept_b, send_b = run_halve(kept_b, got_b)
    kept_a, send_b, acc = tie((kept_a, send_b, acc))
    got_b = along(send_b, 1)
    q_keep, q_send = run_query_last(sc_own, acc, w_uk)
    got_a, q_send = tie((got_a, q_send))
    q_got = to_key(q_send, 1)
    kept_a, send_a = run_halve(kept_a, got_a)
    kept_b, send_a = tie((kept_b, send_a))
    got_a = along(send_a, 2)
    kept_b, send_b = run_halve(kept_b, got_b)
    kept_a, send_b = tie((kept_a, send_b))
    got_b = along(send_b, 2)
    (own_a,) = run_halve(kept_a, got_a)
    kept_b, own_a = tie((kept_b, own_a))
    got_a = along(own_a, 2)
    q_keep, q_send = run_halve(q_keep, q_got)
    got_b, q_send = tie((got_b, q_send))
    q_got = to_key(q_send, 2)
    (own_b,) = run_halve(kept_b, got_b)
    own_a, own_b = tie((own_a, own_b))
    got_b = along(own_b, 2)
    own_a = run_join(own_a, got_a)
    own_b, own_a = tie((own_b, own_a))
    got_a = along(own_a, 1)
    q_keep, q_send = run_halve(q_keep, q_got)
    got_b, q_send = tie((got_b, q_send))
    q_got = to_key(q_send, 4)
    own_b = run_join(own_b, got_b)
    own_a, own_b = tie((own_a, own_b))
    got_b = along(own_b, 1)
    own_a = run_join(own_a, got_a)
    own_b, own_a = tie((own_b, own_a))
    far_a, near_a = along(own_a, 0), to_sibling(own_a)
    q_keep, q_send = run_halve(q_keep, q_got)
    got_b, q_send = tie((got_b, q_send))
    q_got = to_key(q_send, 8)
    own_b = run_join(own_b, got_b)
    far_b, near_b = along(own_b, 0), to_sibling(own_b)
    (dq,) = run_halve(q_keep, q_got)
    pieces = [
        (own_a, far_a, near_a, to_sibling(far_a)),
        (own_b, far_b, near_b, to_sibling(far_b)),
    ]
    d_latent = run_settle(sc_own, *pieces[0], *pieces[1]).T

    d_queries = jnp.transpose(dq.reshape(HEADS, 8, NOPE + ROT), (1, 0, 2))
    return (d_queries, d_latent)


def solution(mesh):
    return jax.shard_map(
        shards,
        mesh=mesh,
        in_specs=(
            P(None, "head", None),
            P("head", None, None),
            P("head", None, None),
            P("key", None),
            P(None, "head", None),
            P(),
        ),
        out_specs=(P("key", "head", None), P("key", None)),
        check_vma=False,
    )
```

```python
import functools
import math

import jax
import jax.numpy as jnp
from jax import lax
from jax.experimental import pallas as pl
from jax.experimental.pallas import tpu as pltpu
from jax.sharding import PartitionSpec as P

bf16 = jnp.bfloat16
f32 = jnp.float32
floor_score = -1e30
floor_top = -1e20

HEADS = 8
ROWS = 128
NOPE = 128
ROT = 64
LAT = 512
WIDE = LAT + ROT
KEYS = 2048
BLK = 256
NBLK = KEYS // BLK
ALL = HEADS * ROWS
PEERS = 16
COLS = WIDE // 4
SCALE = 1.0 / math.sqrt(NOPE + ROT)
SCALE2 = SCALE * math.log2(math.e)
VLIM = 14 * 1024 * 1024
LIMIT_ONE = 34 * 1024 * 1024
LIMIT_TWO = 28 * 1024 * 1024

NT = (((1,), (1,)), ((), ()))


def dot(a, b):
    return jnp.dot(a, b, preferred_element_type=f32)


def dot_nt(a, b):
    return lax.dot_general(a, b, NT, preferred_element_type=f32)


def params(limit=VLIM):
    return pltpu.CompilerParams(vmem_limit_bytes=limit)


in_vmem = pl.BlockSpec(memory_space=pltpu.VMEM)
in_hbm = pl.BlockSpec(memory_space=pltpu.HBM)
in_smem = pl.BlockSpec(memory_space=pltpu.SMEM)


def call(kernel, name, outs, args, scalars=0, scratch=(), limit=VLIM):
    return pl.pallas_call(
        kernel,
        in_specs=[in_smem] * scalars + [in_vmem] * (len(args) - scalars),
        out_specs=[in_vmem] * len(outs),
        out_shape=[jax.ShapeDtypeStruct(shape, kind) for shape, kind in outs],
        scratch_shapes=list(scratch),
        compiler_params=params(limit),
        name=name,
    )(*args)


CHUNK = 256


def pass_one(
    base, off, qt, wuk, wuv, og, lat,
    e_v, dp_v, qcat_t, dlat_t, stat,
    off_v, qt_v, wuk_v, wuv_v, og_v, lat_v, og_wide, qcat, dlat, top, tot, dsum, hide, sem_in,
):
    pairs = ((off, off_v), (qt, qt_v), (wuk, wuk_v), (og, og_v), (wuv, wuv_v), (lat, lat_v))
    loads = [pltpu.make_async_copy(a, b, sem_in.at[k]) for k, (a, b) in enumerate(pairs)]
    for copy in loads:
        copy.start()
    loads[0].wait()
    bound = jnp.broadcast_to(off_v[...], (ROWS, ROWS)).T - base[0]
    bound = jnp.concatenate([bound] * (BLK // 128), axis=1)
    lane = lax.broadcasted_iota(jnp.int32, (ROWS, BLK), 1)
    top[...] = jnp.full((ALL, 128), floor_top, f32)
    tot[...] = jnp.zeros((ALL, 128), f32)
    dsum[...] = jnp.zeros((ALL, 128), f32)
    chunks = [slice(c * CHUNK, (c + 1) * CHUNK) for c in range(ALL // CHUNK)]
    heads = [slice(h * ROWS, (h + 1) * ROWS) for h in range(HEADS)]

    loads[1].wait()
    loads[2].wait()
    for h, rows in enumerate(heads):
        q = qt_v[h].T
        qcat[rows, :LAT] = dot(q[:, :NOPE], wuk_v[h]).astype(bf16)
        qcat[rows, LAT:] = q[:, NOPE:]
    loads[3].wait()
    loads[4].wait()
    og_wide[...] = og_v[...].astype(f32)
    for h, rows in enumerate(heads):
        grad = og_wide[pl.ds(h, ROWS, stride=HEADS), :].astype(bf16)
        dlat[rows, :] = dot_nt(grad, wuv_v[h]).astype(bf16)
    loads[5].wait()
    for rows in heads:
        for k in range(LAT // 128):
            lanes = slice(k * 128, (k + 1) * 128)
            qcat_t[lanes, rows] = qcat[rows, lanes].T
            dlat_t[lanes, rows] = dlat[rows, lanes].T
        qcat_t[LAT:, rows] = qcat[rows, LAT:].T

    def score(j, _):
        at = pl.multiple_of(j * BLK, BLK)
        hide[...] = jnp.where(lane + at <= bound, 0.0, floor_score)
        cols = lat_v[:, pl.ds(at, BLK)]
        for rows in chunks:
            s = dot(qcat[rows, :], cols)
            s = (s.reshape(CHUNK // ROWS, ROWS, BLK) + hide[...][None]).reshape(CHUNK, BLK)
            e_v[j, rows, :] = s
            best = top[rows, :]
            for k in range(BLK // 128):
                best = jnp.maximum(best, s[:, k * 128 : (k + 1) * 128])
            top[rows, :] = best
        return 0

    lax.fori_loop(0, NBLK, score, 0, unroll=NBLK)
    top[...] = jnp.broadcast_to(jnp.max(top[...], axis=1, keepdims=True) * SCALE2, (ALL, 128))

    def weigh(j, _):
        cols = lat_v[:LAT, pl.ds(pl.multiple_of(j * BLK, BLK), BLK)]
        for rows in chunks:
            dp = dot(dlat[rows, :], cols)
            dp_v[j, rows, :] = dp
            s = e_v[j, rows, :]
            m = top[rows, :]
            t, d = tot[rows, :], dsum[rows, :]
            for k in range(BLK // 128):
                lanes = slice(k * 128, (k + 1) * 128)
                e = jnp.exp2(s[:, lanes] * SCALE2 - m)
                e_v[j, rows, lanes] = e
                t = t + e
                d = d + e * dp[:, lanes]
            tot[rows, :] = t
            dsum[rows, :] = d
        return 0

    lax.fori_loop(0, NBLK, weigh, 0, unroll=NBLK)
    near = lane[:, :128]
    for h, rows in enumerate(heads):
        t = jnp.sum(tot[rows, :], axis=1, keepdims=True)
        d = jnp.sum(dsum[rows, :], axis=1, keepdims=True)
        x = jnp.where(near == 0, top[rows, :], jnp.where(near == 1, t, d)).T
        for k in range(3):
            line = x[k : k + 1, :]
            for peer in range(PEERS):
                stat[peer, k * 8 + h : k * 8 + h + 1, :] = line


def run_pass_one(base, offsets, qt, wuk, wuv, og, lat_t):
    big = (NBLK, ALL, BLK)
    outs = [(big, f32), (big, f32), ((WIDE, ALL), bf16), ((LAT, ALL), bf16)]
    outs += [((PEERS, 24, 128), f32)]
    column = pltpu.VMEM((ALL, 128), f32)
    return pl.pallas_call(
        pass_one,
        in_specs=[in_smem] + [in_hbm] * 6,
        out_specs=[in_vmem] * 5,
        out_shape=[jax.ShapeDtypeStruct(shape, kind) for shape, kind in outs],
        scratch_shapes=[pltpu.VMEM(a.shape, a.dtype) for a in (offsets, qt, wuk, wuv, og, lat_t)]
        + [
            column,
            pltpu.VMEM((ALL, WIDE), bf16),
            pltpu.VMEM((ALL, LAT), bf16),
            column,
            column,
            column,
            pltpu.VMEM((ROWS, BLK), f32),
            pltpu.SemaphoreType.DMA((6,)),
        ],
        compiler_params=params(LIMIT_ONE),
        name="pass_one",
    )(base, offsets, qt, wuk, wuv, og, lat_t)


def place(half, r):
    return jnp.where(half == 0, r[0] * 4 + r[1] * 2 + r[2], r[1] * 4 + r[2] * 2 + r[0])


def key_block(r0, chain, sc):
    return sc[3] * 4 + chain * 2 + jnp.bitwise_xor(sc[0], r0)


TALL = 512


def second(chain, sc, coef, delta, qcat_t, dlat_t, e, dp, x_out, ds_out):
    for i in range(2):
        kb = key_block(i, chain, sc)
        scores = values = None
        for c in range(ALL // TALL):
            rows = slice(c * TALL, (c + 1) * TALL)
            cf = jnp.concatenate([coef[rows, :]] * (BLK // 128), axis=1)
            dl = jnp.concatenate([delta[rows, :]] * (BLK // 128), axis=1)
            p = e[kb, rows, :] * cf
            ds = (p * (dp[kb, rows, :] - dl)).astype(bf16)
            ds_out[i, rows, :] = ds
            from_scores = dot(qcat_t[:, rows], ds)
            from_values = dot(dlat_t[:, rows], p.astype(bf16))
            scores = from_scores if c == 0 else scores + from_scores
            values = from_values if c == 0 else values + from_values
        scores = scores * SCALE
        low = (scores[:LAT] + values).astype(bf16)
        high = scores[LAT:].astype(bf16)
        for q in range(4):
            r = (i, jnp.bitwise_xor(sc[1], q & 1), jnp.bitwise_xor(sc[2], q >> 1))
            at = place(sc[3], r)
            if q < 3:
                x_out[at] = low[q * COLS : (q + 1) * COLS]
            else:
                x_out[at, : LAT - 3 * COLS, :] = low[3 * COLS :]
                x_out[at, LAT - 3 * COLS :, :] = high


def second_first(sc, stat, qcat_t, dlat_t, e, dp, x_out, ds_out, coef, delta):
    m = stat[:, 0:8, :]
    best = jnp.max(m, axis=0)
    w = jnp.exp2(m - best[None])
    total = jnp.sum(w * stat[:, 8:16, :], axis=0)
    dtotal = jnp.sum(w * stat[:, 16:24, :], axis=0)
    cf = jnp.exp2(stat[sc[4], 0:8, :] - best) / total
    dl = dtotal / total
    for h in range(HEADS):
        rows = slice(h * ROWS, (h + 1) * ROWS)
        coef[rows, :] = jnp.broadcast_to(cf[h : h + 1], (128, 128)).T
        delta[rows, :] = jnp.broadcast_to(dl[h : h + 1], (128, 128)).T
    second(0, sc, coef, delta, qcat_t, dlat_t, e, dp, x_out, ds_out)


def run_second(sc, heads_in, qcat_t, dlat_t, e, dp, chain):
    first = len(heads_in) == 1
    outs = [((8, COLS, BLK), bf16), ((2, ALL, BLK), bf16)]
    if first:
        outs += [((ALL, 128), f32)] * 2
    return call(
        second_first if first else functools.partial(second, chain),
        "second_first" if first else "second",
        outs,
        (sc, *heads_in, qcat_t, dlat_t, e, dp),
        1,
        limit=LIMIT_TWO,
    )


def query_piece(chain, sc, ds, lat, *refs):
    total = None if len(refs) == 1 else refs[0][...]
    for i in range(2):
        kb = key_block(i, chain, sc)
        part = dot_nt(ds[i], lat[:, pl.ds(pl.multiple_of(kb * BLK, BLK), BLK)])
        total = part if total is None else total + part
    refs[-1][...] = total


def run_query_piece(chain, sc, ds, lat_t, *acc):
    kernel = functools.partial(query_piece, chain)
    return call(kernel, "query_piece", [((ALL, WIDE), f32)], (sc, ds, lat_t, *acc), 1)[0]


def query_last(acc, wuk, out, wide):
    for h in range(HEADS):
        rows = slice(h * ROWS, (h + 1) * ROWS)
        x = acc[rows, :LAT] * SCALE
        hi = x.astype(bf16)
        lo = (x - hi.astype(f32)).astype(bf16)
        wide[h, :, :NOPE] = dot_nt(hi, wuk[h]) + dot_nt(lo, wuk[h])
        wide[h, :, NOPE:] = acc[rows, LAT:] * SCALE
    for g in range(PEERS):
        out[g] = wide[:, g * 8 : (g + 1) * 8, :].reshape(HEADS * 8, NOPE + ROT).astype(bf16)


def run_query_last(acc, wuk):
    outs = [((PEERS, HEADS * 8, NOPE + ROT), bf16)]
    scratch = [pltpu.VMEM((HEADS, ROWS, NOPE + ROT), f32)]
    return call(query_last, "query_last", outs, (acc, wuk), 0, scratch)[0]


def halve(kept, got, *outs):
    n = kept.shape[0]
    for k in range(n):
        total = (kept[k].astype(f32) + got[k].astype(f32)).astype(bf16)
        outs[k * len(outs) // n][k % (n // len(outs))] = total


def run_halve(kept, got):
    n = kept.shape[0]
    outs = [((max(n // 2, 1), *kept.shape[1:]), bf16)] * min(n, 2)
    return call(halve, "halve", outs, (kept, got))


def join(own, got, out):
    n = own.shape[0]
    out[:n] = own[...]
    out[n:] = got[...]


def run_join(own, got):
    return call(join, "join", [((2 * own.shape[0], COLS, BLK), bf16)], (own, got))[0]


def settle(chain, sc, mine, mine_far, other, other_far, *refs):
    out, sem = refs[-2:]
    copies = []
    for near, far, half in ((mine, mine_far, sc[3]), (other, other_far, 1 - sc[3])):
        for i in range(8):
            b = (i >> 2 & 1, i >> 1 & 1, i & 1)
            r = [jnp.where(half == 0, b[d], b[(d + 2) % 3]) for d in range(3)]
            a = [jnp.bitwise_xor(sc[d], r[d]) for d in range(3)]
            rows = pl.ds(pl.multiple_of((a[2] * 2 + a[1]) * COLS, 16), COLS)
            lanes = pl.ds(pl.multiple_of((half * 4 + chain * 2 + a[0]) * BLK, BLK), BLK)
            block = near.at[i] if i < 4 else far.at[i - 4]
            copy = pltpu.make_async_copy(block, out.at[rows, lanes], sem.at[len(copies)])
            copy.start()
            copies.append(copy)
    for copy in copies:
        copy.wait()


def run_settle(chain, sc, pieces, *earlier):
    return pl.pallas_call(
        functools.partial(settle, chain),
        in_specs=[in_smem] + [in_vmem] * len(pieces) + [in_hbm] * len(earlier),
        out_specs=in_hbm,
        out_shape=jax.ShapeDtypeStruct((WIDE, KEYS), bf16),
        scratch_shapes=[pltpu.SemaphoreType.DMA((16,))],
        input_output_aliases={5: 0} if earlier else {},
        compiler_params=params(),
        name="settle",
    )(sc, *pieces, *earlier)


def cube_neighbour(k, d):
    y, rest = k >> 2, k & 3
    if d == 2:
        return k ^ 2
    gray = (y ^ (y >> 1)) ^ (1 << d)
    back = gray ^ (gray >> 1)
    return back * 4 + rest


def along(value, n):
    pairs = [(k, cube_neighbour(k, (n + (k & 1)) % 3)) for k in range(16)]
    return lax.ppermute(value, "head", pairs)


def to_sibling(value):
    return lax.ppermute(value, "head", [(k, k ^ 1) for k in range(16)])


def held(value):
    return pltpu.with_memory_space_constraint(value, pltpu.HBM)


def shards(queries, w_uk, w_uv, latent, out_grad, offsets):
    head = lax.axis_index("head").astype(jnp.int32)
    key = lax.axis_index("key").astype(jnp.int32)
    y = head >> 2
    gray = y ^ (y >> 1)
    core = head & 1
    sc_own = jnp.stack([gray & 1, gray >> 1, (head >> 1) & 1, core, key])
    sc_far = jnp.stack([gray & 1, gray >> 1, (head >> 1) & 1, 1 - core, key])
    lat_t = latent.T
    qt = jnp.transpose(queries, (1, 2, 0))
    og = out_grad.reshape(ALL, 128)
    e, dp, qcat_t, dlat_t, stat = run_pass_one(
        (key * KEYS)[None], *map(held, (offsets[None], qt, w_uk, w_uv, og, lat_t))
    )
    stat, sc_own, sc_far = lax.optimization_barrier((stat, sc_own, sc_far))
    stat = lax.all_to_all(stat, "key", 0, 0, tiled=True)
    turned = (qcat_t, dlat_t, e, dp)
    x_far, far_a, coef, delta = run_second(sc_far, (stat,), *turned, 0)
    came = to_sibling(x_far)
    x_own, own_a = run_second(sc_own, (coef, delta), *turned, 0)
    kept_a, send_a = run_halve(x_own, came)
    tie = lax.optimization_barrier
    sc_late, send_a = tie((sc_far, send_a))
    got_a = along(send_a, 0)
    x_far, far_b = run_second(sc_late, (coef, delta), *turned, 1)
    came = to_sibling(x_far)
    x_own, own_b = run_second(sc_own, (coef, delta), *turned, 1)
    kept_b, send_b = run_halve(x_own, came)
    got_b = along(send_b, 0)
    acc = run_query_piece(0, sc_far, far_a, lat_t)
    acc = run_query_piece(0, sc_own, own_a, lat_t, acc)
    got_a, acc = tie((got_a, acc))
    kept_a, send_a = run_halve(kept_a, got_a)
    kept_b, send_a, acc = tie((kept_b, send_a, acc))
    got_a = along(send_a, 1)
    acc = run_query_piece(1, sc_far, far_b, lat_t, acc)
    acc = run_query_piece(1, sc_own, own_b, lat_t, acc)
    got_b, acc = tie((got_b, acc))
    kept_b, send_b = run_halve(kept_b, got_b)
    kept_a, send_b, acc = tie((kept_a, send_b, acc))
    got_b = along(send_b, 1)
    dq = run_query_last(acc, w_uk)
    got_a, dq = tie((got_a, dq))
    dq = lax.all_to_all(dq, "key", 0, 0, tiled=True)
    kept_a, send_a = run_halve(kept_a, got_a)
    kept_b, send_a = tie((kept_b, send_a))
    got_a = along(send_a, 2)
    kept_b, send_b = run_halve(kept_b, got_b)
    kept_a, send_b = tie((kept_a, send_b))
    got_b = along(send_b, 2)
    (own_a,) = run_halve(kept_a, got_a)
    kept_b, own_a = tie((kept_b, own_a))
    got_a = along(own_a, 2)
    (own_b,) = run_halve(kept_b, got_b)
    own_a, own_b = tie((own_a, own_b))
    got_b = along(own_b, 2)
    own_a = run_join(own_a, got_a)
    own_b, own_a = tie((own_b, own_a))
    got_a = along(own_a, 1)
    own_b = run_join(own_b, got_b)
    own_a, own_b, dq = tie((own_a, own_b, dq))
    got_b = along(own_b, 1)
    own_a = run_join(own_a, got_a)
    own_b, own_a = tie((own_b, own_a))
    far_a, near_a = along(own_a, 0), to_sibling(own_a)
    own_b = run_join(own_b, got_b)
    far_b, near_b = along(own_b, 0), to_sibling(own_b)
    pieces = [
        (own_a, far_a, near_a, to_sibling(far_a)),
        (own_b, far_b, near_b, to_sibling(far_b)),
    ]
    d_latent = run_settle(1, sc_own, pieces[1], run_settle(0, sc_own, pieces[0])).T

    dq = jnp.sum(dq.astype(f32), axis=0).astype(bf16)
    d_queries = jnp.transpose(dq.reshape(HEADS, 8, NOPE + ROT), (1, 0, 2))
    return (d_queries, d_latent)


def solution(mesh):
    return jax.shard_map(
        shards,
        mesh=mesh,
        in_specs=(
            P(None, "head", None),
            P("head", None, None),
            P("head", None, None),
            P("key", None),
            P(None, "head", None),
            P(),
        ),
        out_specs=(P("key", "head", None), P("key", None)),
        check_vma=False,
    )
```

```python
import functools
import math

import jax
import jax.numpy as jnp
from jax import lax
from jax.experimental import pallas as pl
from jax.experimental.pallas import tpu as pltpu
from jax.sharding import PartitionSpec as P

bf16 = jnp.bfloat16
f32 = jnp.float32
floor_score = -1e30
floor_top = -1e20

HEADS = 8
ROWS = 128
NOPE = 128
ROT = 64
LAT = 512
WIDE = LAT + ROT
KEYS = 2048
BLK = 256
NBLK = KEYS // BLK
ALL = HEADS * ROWS
PEERS = 16
COLS = WIDE // 4
SCALE = 1.0 / math.sqrt(NOPE + ROT)
SCALE2 = SCALE * math.log2(math.e)
VLIM = 14 * 1024 * 1024
LIMIT_ONE = 34 * 1024 * 1024
LIMIT_TWO = 28 * 1024 * 1024

NT = (((1,), (1,)), ((), ()))


def dot(a, b):
    return jnp.dot(a, b, preferred_element_type=f32)


def dot_nt(a, b):
    return lax.dot_general(a, b, NT, preferred_element_type=f32)


def params(limit=VLIM):
    return pltpu.CompilerParams(vmem_limit_bytes=limit)


in_vmem = pl.BlockSpec(memory_space=pltpu.VMEM)
in_hbm = pl.BlockSpec(memory_space=pltpu.HBM)
in_smem = pl.BlockSpec(memory_space=pltpu.SMEM)


def call(kernel, name, outs, args, scalars=0, scratch=(), limit=VLIM):
    return pl.pallas_call(
        kernel,
        in_specs=[in_smem] * scalars + [in_vmem] * (len(args) - scalars),
        out_specs=[in_vmem] * len(outs),
        out_shape=[jax.ShapeDtypeStruct(shape, kind) for shape, kind in outs],
        scratch_shapes=list(scratch),
        compiler_params=params(limit),
        name=name,
    )(*args)


CHUNK = 256


def pass_one(
    base, off, qt, wuk, wuv, og, lat,
    e_v, dp_v, qcat_t, dlat_t, stat,
    off_v, qt_v, wuk_v, wuv_v, og_v, lat_v, og_wide, qcat, dlat, top, tot, dsum, hide, sem_in,
):
    pairs = ((off, off_v), (qt, qt_v), (wuk, wuk_v), (og, og_v), (wuv, wuv_v), (lat, lat_v))
    loads = [pltpu.make_async_copy(a, b, sem_in.at[k]) for k, (a, b) in enumerate(pairs)]
    for copy in loads:
        copy.start()
    loads[0].wait()
    bound = jnp.broadcast_to(off_v[...], (ROWS, ROWS)).T - base[0]
    bound = jnp.concatenate([bound] * (BLK // 128), axis=1)
    lane = lax.broadcasted_iota(jnp.int32, (ROWS, BLK), 1)
    top[...] = jnp.full((ALL, 128), floor_top, f32)
    tot[...] = jnp.zeros((ALL, 128), f32)
    dsum[...] = jnp.zeros((ALL, 128), f32)
    chunks = [slice(c * CHUNK, (c + 1) * CHUNK) for c in range(ALL // CHUNK)]
    heads = [slice(h * ROWS, (h + 1) * ROWS) for h in range(HEADS)]

    loads[1].wait()
    loads[2].wait()
    for h, rows in enumerate(heads):
        q = qt_v[h].T
        qcat[rows, :LAT] = dot(q[:, :NOPE], wuk_v[h]).astype(bf16)
        qcat[rows, LAT:] = q[:, NOPE:]
    loads[3].wait()
    loads[4].wait()
    og_wide[...] = og_v[...].astype(f32)
    for h, rows in enumerate(heads):
        grad = og_wide[pl.ds(h, ROWS, stride=HEADS), :].astype(bf16)
        dlat[rows, :] = dot_nt(grad, wuv_v[h]).astype(bf16)
    loads[5].wait()
    for rows in heads:
        for k in range(LAT // 128):
            lanes = slice(k * 128, (k + 1) * 128)
            qcat_t[lanes, rows] = qcat[rows, lanes].T
            dlat_t[lanes, rows] = dlat[rows, lanes].T
        qcat_t[LAT:, rows] = qcat[rows, LAT:].T

    def score(j, _):
        at = pl.multiple_of(j * BLK, BLK)
        hide[...] = jnp.where(lane + at <= bound, 0.0, floor_score)
        cols = lat_v[:, pl.ds(at, BLK)]
        for rows in chunks:
            s = dot(qcat[rows, :], cols)
            s = (s.reshape(CHUNK // ROWS, ROWS, BLK) + hide[...][None]).reshape(CHUNK, BLK)
            e_v[j, rows, :] = s
            best = top[rows, :]
            for k in range(BLK // 128):
                best = jnp.maximum(best, s[:, k * 128 : (k + 1) * 128])
            top[rows, :] = best
        return 0

    lax.fori_loop(0, NBLK, score, 0, unroll=NBLK)
    top[...] = jnp.broadcast_to(jnp.max(top[...], axis=1, keepdims=True) * SCALE2, (ALL, 128))

    def weigh(j, _):
        cols = lat_v[:LAT, pl.ds(pl.multiple_of(j * BLK, BLK), BLK)]
        for rows in chunks:
            dp = dot(dlat[rows, :], cols)
            dp_v[j, rows, :] = dp
            s = e_v[j, rows, :]
            m = top[rows, :]
            t, d = tot[rows, :], dsum[rows, :]
            for k in range(BLK // 128):
                lanes = slice(k * 128, (k + 1) * 128)
                e = jnp.exp2(s[:, lanes] * SCALE2 - m)
                e_v[j, rows, lanes] = e
                t = t + e
                d = d + e * dp[:, lanes]
            tot[rows, :] = t
            dsum[rows, :] = d
        return 0

    lax.fori_loop(0, NBLK, weigh, 0, unroll=NBLK)
    near = lane[:, :128]
    for h, rows in enumerate(heads):
        t = jnp.sum(tot[rows, :], axis=1, keepdims=True)
        d = jnp.sum(dsum[rows, :], axis=1, keepdims=True)
        x = jnp.where(near == 0, top[rows, :], jnp.where(near == 1, t, d)).T
        for k in range(3):
            line = x[k : k + 1, :]
            for peer in range(PEERS):
                stat[peer, k * 8 + h : k * 8 + h + 1, :] = line


def run_pass_one(base, offsets, qt, wuk, wuv, og, lat_t):
    big = (NBLK, ALL, BLK)
    outs = [(big, f32), (big, f32), ((WIDE, ALL), bf16), ((LAT, ALL), bf16)]
    outs += [((PEERS, 24, 128), f32)]
    column = pltpu.VMEM((ALL, 128), f32)
    return pl.pallas_call(
        pass_one,
        in_specs=[in_smem] + [in_hbm] * 6,
        out_specs=[in_vmem] * 5,
        out_shape=[jax.ShapeDtypeStruct(shape, kind) for shape, kind in outs],
        scratch_shapes=[pltpu.VMEM(a.shape, a.dtype) for a in (offsets, qt, wuk, wuv, og, lat_t)]
        + [
            column,
            pltpu.VMEM((ALL, WIDE), bf16),
            pltpu.VMEM((ALL, LAT), bf16),
            column,
            column,
            column,
            pltpu.VMEM((ROWS, BLK), f32),
            pltpu.SemaphoreType.DMA((6,)),
        ],
        compiler_params=params(LIMIT_ONE),
        name="pass_one",
    )(base, offsets, qt, wuk, wuv, og, lat_t)


def place(half, r):
    return jnp.where(half == 0, r[0] * 4 + r[1] * 2 + r[2], r[1] * 4 + r[2] * 2 + r[0])


def key_block(r0, chain, sc):
    return sc[3] * 4 + chain * 2 + jnp.bitwise_xor(sc[0], r0)


TALL = 512


def second(chain, sc, coef, delta, qcat_t, dlat_t, e, dp, x_out, ds_out):
    for i in range(2):
        kb = key_block(i, chain, sc)
        scores = values = None
        for c in range(ALL // TALL):
            rows = slice(c * TALL, (c + 1) * TALL)
            cf = jnp.concatenate([coef[rows, :]] * (BLK // 128), axis=1)
            dl = jnp.concatenate([delta[rows, :]] * (BLK // 128), axis=1)
            p = e[kb, rows, :] * cf
            ds = (p * (dp[kb, rows, :] - dl)).astype(bf16)
            ds_out[i, rows, :] = ds
            from_scores = dot(qcat_t[:, rows], ds)
            from_values = dot(dlat_t[:, rows], p.astype(bf16))
            scores = from_scores if c == 0 else scores + from_scores
            values = from_values if c == 0 else values + from_values
        scores = scores * SCALE
        low = (scores[:LAT] + values).astype(bf16)
        high = scores[LAT:].astype(bf16)
        for q in range(4):
            r = (i, jnp.bitwise_xor(sc[1], q & 1), jnp.bitwise_xor(sc[2], q >> 1))
            at = place(sc[3], r)
            if q < 3:
                x_out[at] = low[q * COLS : (q + 1) * COLS]
            else:
                x_out[at, : LAT - 3 * COLS, :] = low[3 * COLS :]
                x_out[at, LAT - 3 * COLS :, :] = high


def second_first(sc, stat, qcat_t, dlat_t, e, dp, x_out, ds_out, coef, delta):
    m = stat[:, 0:8, :]
    best = jnp.max(m, axis=0)
    w = jnp.exp2(m - best[None])
    total = jnp.sum(w * stat[:, 8:16, :], axis=0)
    dtotal = jnp.sum(w * stat[:, 16:24, :], axis=0)
    cf = jnp.exp2(stat[sc[4], 0:8, :] - best) / total
    dl = dtotal / total
    for h in range(HEADS):
        rows = slice(h * ROWS, (h + 1) * ROWS)
        coef[rows, :] = jnp.broadcast_to(cf[h : h + 1], (128, 128)).T
        delta[rows, :] = jnp.broadcast_to(dl[h : h + 1], (128, 128)).T
    second(0, sc, coef, delta, qcat_t, dlat_t, e, dp, x_out, ds_out)


def run_second(sc, heads_in, qcat_t, dlat_t, e, dp, chain):
    first = len(heads_in) == 1
    outs = [((8, COLS, BLK), bf16), ((2, ALL, BLK), bf16)]
    if first:
        outs += [((ALL, 128), f32)] * 2
    return call(
        second_first if first else functools.partial(second, chain),
        "second_first" if first else "second",
        outs,
        (sc, *heads_in, qcat_t, dlat_t, e, dp),
        1,
        limit=LIMIT_TWO,
    )


def query_piece(chain, sc, ds, lat, *refs):
    total = None if len(refs) == 1 else refs[0][...]
    for i in range(2):
        kb = key_block(i, chain, sc)
        part = dot_nt(ds[i], lat[:, pl.ds(pl.multiple_of(kb * BLK, BLK), BLK)])
        total = part if total is None else total + part
    refs[-1][...] = total


def run_query_piece(chain, sc, ds, lat_t, *acc):
    kernel = functools.partial(query_piece, chain)
    return call(kernel, "query_piece", [((ALL, WIDE), f32)], (sc, ds, lat_t, *acc), 1)[0]


def query_last(acc, wuk, out, wide):
    for h in range(HEADS):
        rows = slice(h * ROWS, (h + 1) * ROWS)
        x = acc[rows, :LAT] * SCALE
        hi = x.astype(bf16)
        lo = (x - hi.astype(f32)).astype(bf16)
        wide[h, :, :NOPE] = dot_nt(hi, wuk[h]) + dot_nt(lo, wuk[h])
        wide[h, :, NOPE:] = acc[rows, LAT:] * SCALE
    for g in range(PEERS):
        out[g] = wide[:, g * 8 : (g + 1) * 8, :].reshape(HEADS * 8, NOPE + ROT).astype(bf16)


def run_query_last(acc, wuk):
    outs = [((PEERS, HEADS * 8, NOPE + ROT), bf16)]
    scratch = [pltpu.VMEM((HEADS, ROWS, NOPE + ROT), f32)]
    return call(query_last, "query_last", outs, (acc, wuk), 0, scratch)[0]


def halve(kept, got, *outs):
    n = kept.shape[0]
    for k in range(n):
        total = (kept[k].astype(f32) + got[k].astype(f32)).astype(bf16)
        outs[k * len(outs) // n][k % (n // len(outs))] = total


def run_halve(kept, got):
    n = kept.shape[0]
    outs = [((max(n // 2, 1), *kept.shape[1:]), bf16)] * min(n, 2)
    return call(halve, "halve", outs, (kept, got))


def quarter(kept_a, got_a, kept_b, got_b, keep, first, second_, both):
    for c, (kept, got) in enumerate(((kept_a, got_a), (kept_b, got_b))):
        for k, out in enumerate((keep, second_, first, both)):
            out[c] = (kept[k].astype(f32) + got[k].astype(f32)).astype(bf16)


def run_quarter(*args):
    return call(quarter, "quarter", [((2, COLS, BLK), bf16)] * 4, args)


def whole_sum(keep, first, second_, both, out):
    total = keep[...].astype(f32) + first[...].astype(f32)
    out[...] = (total + (second_[...].astype(f32) + both[...].astype(f32))).astype(bf16)


def run_whole_sum(*args):
    return call(whole_sum, "whole_sum", [((2, COLS, BLK), bf16)], args)[0]


def join(own, first, second_, both, *outs):
    for k, part in enumerate((own, second_, first, both)):
        for c, out in enumerate(outs):
            out[k] = part[c]


def run_join(*args):
    return call(join, "join", [((4, COLS, BLK), bf16)] * 2, args)


def settle(chain, sc, mine, mine_far, other, other_far, *refs):
    out, sem = refs[-2:]
    copies = []
    for near, far, half in ((mine, mine_far, sc[3]), (other, other_far, 1 - sc[3])):
        for i in range(8):
            b = (i >> 2 & 1, i >> 1 & 1, i & 1)
            r = [jnp.where(half == 0, b[d], b[(d + 2) % 3]) for d in range(3)]
            a = [jnp.bitwise_xor(sc[d], r[d]) for d in range(3)]
            rows = pl.ds(pl.multiple_of((a[2] * 2 + a[1]) * COLS, 16), COLS)
            lanes = pl.ds(pl.multiple_of((half * 4 + chain * 2 + a[0]) * BLK, BLK), BLK)
            block = near.at[i] if i < 4 else far.at[i - 4]
            copy = pltpu.make_async_copy(block, out.at[rows, lanes], sem.at[len(copies)])
            copy.start()
            copies.append(copy)
    for copy in copies:
        copy.wait()


def run_settle(chain, sc, pieces, *earlier):
    return pl.pallas_call(
        functools.partial(settle, chain),
        in_specs=[in_smem] + [in_vmem] * len(pieces) + [in_hbm] * len(earlier),
        out_specs=in_hbm,
        out_shape=jax.ShapeDtypeStruct((WIDE, KEYS), bf16),
        scratch_shapes=[pltpu.SemaphoreType.DMA((16,))],
        input_output_aliases={5: 0} if earlier else {},
        compiler_params=params(),
        name="settle",
    )(sc, *pieces, *earlier)


def cube_neighbour(k, d):
    y, rest = k >> 2, k & 3
    if d == 2:
        return k ^ 2
    gray = (y ^ (y >> 1)) ^ (1 << d)
    back = gray ^ (gray >> 1)
    return back * 4 + rest


def along(value, n):
    pairs = [(k, cube_neighbour(k, (n + (k & 1)) % 3)) for k in range(16)]
    return lax.ppermute(value, "head", pairs)


def to_three(values):
    got = []
    for value, flips in zip(values, ((1,), (2,), (1, 2))):
        pairs = []
        for k in range(16):
            other = k
            for n in flips:
                other = cube_neighbour(other, (n + (k & 1)) % 3)
            pairs.append((k, other))
        got.append(lax.ppermute(value, "head", pairs))
    return got


def to_sibling(value):
    return lax.ppermute(value, "head", [(k, k ^ 1) for k in range(16)])


def held(value):
    return pltpu.with_memory_space_constraint(value, pltpu.HBM)


def shards(queries, w_uk, w_uv, latent, out_grad, offsets):
    head = lax.axis_index("head").astype(jnp.int32)
    key = lax.axis_index("key").astype(jnp.int32)
    y = head >> 2
    gray = y ^ (y >> 1)
    core = head & 1
    sc_own = jnp.stack([gray & 1, gray >> 1, (head >> 1) & 1, core, key])
    sc_far = jnp.stack([gray & 1, gray >> 1, (head >> 1) & 1, 1 - core, key])
    lat_t = latent.T
    qt = jnp.transpose(queries, (1, 2, 0))
    og = out_grad.reshape(ALL, 128)
    e, dp, qcat_t, dlat_t, stat = run_pass_one(
        (key * KEYS)[None], *map(held, (offsets[None], qt, w_uk, w_uv, og, lat_t))
    )
    stat, sc_own, sc_far = lax.optimization_barrier((stat, sc_own, sc_far))
    stat = lax.all_to_all(stat, "key", 0, 0, tiled=True)
    turned = (qcat_t, dlat_t, e, dp)
    x_far, far_a, coef, delta = run_second(sc_far, (stat,), *turned, 0)
    came = to_sibling(x_far)
    x_own, own_a = run_second(sc_own, (coef, delta), *turned, 0)
    kept_a, send_a = run_halve(x_own, came)
    tie = lax.optimization_barrier
    sc_late, send_a = tie((sc_far, send_a))
    got_a = along(send_a, 0)
    x_far, far_b = run_second(sc_late, (coef, delta), *turned, 1)
    came = to_sibling(x_far)
    x_own, own_b = run_second(sc_own, (coef, delta), *turned, 1)
    kept_b, send_b = run_halve(x_own, came)
    got_b = along(send_b, 0)
    acc = run_query_piece(0, sc_far, far_a, lat_t)
    acc = run_query_piece(0, sc_own, own_a, lat_t, acc)
    acc = run_query_piece(1, sc_far, far_b, lat_t, acc)
    acc = run_query_piece(1, sc_own, own_b, lat_t, acc)
    got_b, acc = tie((got_b, acc))
    keep, *sends = run_quarter(kept_a, got_a, kept_b, got_b)
    *sends, acc = tie((*sends, acc))
    got = to_three(sends)
    dq = run_query_last(acc, w_uk)
    dq = lax.all_to_all(dq, "key", 0, 0, tiled=True)
    own = run_whole_sum(keep, *got)
    own_a, own_b = run_join(own, *to_three([own] * 3))
    own_a, own_b, dq = tie((own_a, own_b, dq))
    far_a, near_a = along(own_a, 0), to_sibling(own_a)
    far_b, near_b = along(own_b, 0), to_sibling(own_b)
    pieces = [
        (own_a, far_a, near_a, to_sibling(far_a)),
        (own_b, far_b, near_b, to_sibling(far_b)),
    ]
    d_latent = run_settle(1, sc_own, pieces[1], run_settle(0, sc_own, pieces[0])).T

    dq = jnp.sum(dq.astype(f32), axis=0).astype(bf16)
    d_queries = jnp.transpose(dq.reshape(HEADS, 8, NOPE + ROT), (1, 0, 2))
    return (d_queries, d_latent)


def solution(mesh):
    return jax.shard_map(
        shards,
        mesh=mesh,
        in_specs=(
            P(None, "head", None),
            P("head", None, None),
            P("head", None, None),
            P("key", None),
            P(None, "head", None),
            P(),
        ),
        out_specs=(P("key", "head", None), P("key", None)),
        check_vma=False,
    )
```

```python
import functools
import math

import jax
import jax.numpy as jnp
from jax import lax
from jax.experimental import pallas as pl
from jax.experimental.pallas import tpu as pltpu
from jax.sharding import PartitionSpec as P

bf16 = jnp.bfloat16
f32 = jnp.float32
floor_score = -1e30
floor_top = -1e20

HEADS = 8
ROWS = 128
NOPE = 128
ROT = 64
LAT = 512
WIDE = LAT + ROT
KEYS = 2048
BLK = 256
NBLK = KEYS // BLK
ALL = HEADS * ROWS
PEERS = 16
COLS = WIDE // 4
SCALE = 1.0 / math.sqrt(NOPE + ROT)
SCALE2 = SCALE * math.log2(math.e)
VLIM = 14 * 1024 * 1024
LIMIT_ONE = 34 * 1024 * 1024
LIMIT_TWO = 28 * 1024 * 1024

NT = (((1,), (1,)), ((), ()))


def dot(a, b):
    return jnp.dot(a, b, preferred_element_type=f32)


def dot_nt(a, b):
    return lax.dot_general(a, b, NT, preferred_element_type=f32)


def params(limit=VLIM):
    return pltpu.CompilerParams(vmem_limit_bytes=limit)


in_vmem = pl.BlockSpec(memory_space=pltpu.VMEM)
in_hbm = pl.BlockSpec(memory_space=pltpu.HBM)
in_smem = pl.BlockSpec(memory_space=pltpu.SMEM)


def call(kernel, name, outs, args, scalars=0, scratch=(), limit=VLIM):
    return pl.pallas_call(
        kernel,
        in_specs=[in_smem] * scalars + [in_vmem] * (len(args) - scalars),
        out_specs=[in_vmem] * len(outs),
        out_shape=[jax.ShapeDtypeStruct(shape, kind) for shape, kind in outs],
        scratch_shapes=list(scratch),
        compiler_params=params(limit),
        name=name,
    )(*args)


CHUNK = 256


def pass_one(
    base, off, qt, wuk, wuv, og, lat,
    e_v, dp_v, qcat_t, dlat_t, stat,
    off_v, qt_v, wuk_v, wuv_v, og_v, lat_v, og_wide, qcat, dlat, top, tot, dsum, hide, sem_in,
):
    pairs = ((off, off_v), (qt, qt_v), (wuk, wuk_v), (og, og_v), (wuv, wuv_v), (lat, lat_v))
    loads = [pltpu.make_async_copy(a, b, sem_in.at[k]) for k, (a, b) in enumerate(pairs)]
    for copy in loads:
        copy.start()
    loads[0].wait()
    bound = jnp.broadcast_to(off_v[...], (ROWS, ROWS)).T - base[0]
    bound = jnp.concatenate([bound] * (BLK // 128), axis=1)
    lane = lax.broadcasted_iota(jnp.int32, (ROWS, BLK), 1)
    top[...] = jnp.full((ALL, 128), floor_top, f32)
    tot[...] = jnp.zeros((ALL, 128), f32)
    dsum[...] = jnp.zeros((ALL, 128), f32)
    chunks = [slice(c * CHUNK, (c + 1) * CHUNK) for c in range(ALL // CHUNK)]
    heads = [slice(h * ROWS, (h + 1) * ROWS) for h in range(HEADS)]

    loads[1].wait()
    loads[2].wait()
    for h, rows in enumerate(heads):
        q = qt_v[h].T
        qcat[rows, :LAT] = dot(q[:, :NOPE], wuk_v[h]).astype(bf16)
        qcat[rows, LAT:] = q[:, NOPE:]
    loads[3].wait()
    loads[4].wait()
    og_wide[...] = og_v[...].astype(f32)
    for h, rows in enumerate(heads):
        grad = og_wide[pl.ds(h, ROWS, stride=HEADS), :].astype(bf16)
        dlat[rows, :] = dot_nt(grad, wuv_v[h]).astype(bf16)
    loads[5].wait()
    for rows in heads:
        for k in range(LAT // 128):
            lanes = slice(k * 128, (k + 1) * 128)
            qcat_t[lanes, rows] = qcat[rows, lanes].T
            dlat_t[lanes, rows] = dlat[rows, lanes].T
        qcat_t[LAT:, rows] = qcat[rows, LAT:].T

    def score(j, _):
        at = pl.multiple_of(j * BLK, BLK)
        hide[...] = jnp.where(lane + at <= bound, 0.0, floor_score)
        cols = lat_v[:, pl.ds(at, BLK)]
        for rows in chunks:
            s = dot(qcat[rows, :], cols)
            s = (s.reshape(CHUNK // ROWS, ROWS, BLK) + hide[...][None]).reshape(CHUNK, BLK)
            e_v[j, rows, :] = s
            best = top[rows, :]
            for k in range(BLK // 128):
                best = jnp.maximum(best, s[:, k * 128 : (k + 1) * 128])
            top[rows, :] = best
        return 0

    lax.fori_loop(0, NBLK, score, 0, unroll=NBLK)
    top[...] = jnp.broadcast_to(jnp.max(top[...], axis=1, keepdims=True) * SCALE2, (ALL, 128))

    def weigh(j, _):
        cols = lat_v[:LAT, pl.ds(pl.multiple_of(j * BLK, BLK), BLK)]
        for rows in chunks:
            dp = dot(dlat[rows, :], cols)
            dp_v[j, rows, :] = dp
            s = e_v[j, rows, :]
            m = top[rows, :]
            t, d = tot[rows, :], dsum[rows, :]
            for k in range(BLK // 128):
                lanes = slice(k * 128, (k + 1) * 128)
                e = jnp.exp2(s[:, lanes] * SCALE2 - m)
                e_v[j, rows, lanes] = e
                t = t + e
                d = d + e * dp[:, lanes]
            tot[rows, :] = t
            dsum[rows, :] = d
        return 0

    lax.fori_loop(0, NBLK, weigh, 0, unroll=NBLK)
    near = lane[:, :128]
    for h, rows in enumerate(heads):
        t = jnp.sum(tot[rows, :], axis=1, keepdims=True)
        d = jnp.sum(dsum[rows, :], axis=1, keepdims=True)
        x = jnp.where(near == 0, top[rows, :], jnp.where(near == 1, t, d)).T
        for k in range(3):
            line = x[k : k + 1, :]
            for peer in range(PEERS):
                stat[peer, k * 8 + h : k * 8 + h + 1, :] = line


def run_pass_one(base, offsets, qt, wuk, wuv, og, lat_t):
    big = (NBLK, ALL, BLK)
    outs = [(big, f32), (big, f32), ((WIDE, ALL), bf16), ((LAT, ALL), bf16)]
    outs += [((PEERS, 24, 128), f32)]
    column = pltpu.VMEM((ALL, 128), f32)
    return pl.pallas_call(
        pass_one,
        in_specs=[in_smem] + [in_hbm] * 6,
        out_specs=[in_vmem] * 5,
        out_shape=[jax.ShapeDtypeStruct(shape, kind) for shape, kind in outs],
        scratch_shapes=[pltpu.VMEM(a.shape, a.dtype) for a in (offsets, qt, wuk, wuv, og, lat_t)]
        + [
            column,
            pltpu.VMEM((ALL, WIDE), bf16),
            pltpu.VMEM((ALL, LAT), bf16),
            column,
            column,
            column,
            pltpu.VMEM((ROWS, BLK), f32),
            pltpu.SemaphoreType.DMA((6,)),
        ],
        compiler_params=params(LIMIT_ONE),
        name="pass_one",
    )(base, offsets, qt, wuk, wuv, og, lat_t)


def place(half, r):
    return jnp.where(half == 0, r[0] * 4 + r[1] * 2 + r[2], r[1] * 4 + r[2] * 2 + r[0])


def key_block(r0, chain, sc):
    return sc[3] * 4 + chain * 2 + jnp.bitwise_xor(sc[0], r0)


TALL = 512


def second(chain, sc, coef, delta, qcat_t, dlat_t, e, dp, x_out, ds_out):
    for i in range(2):
        kb = key_block(i, chain, sc)
        scores = values = None
        for c in range(ALL // TALL):
            rows = slice(c * TALL, (c + 1) * TALL)
            cf = jnp.concatenate([coef[rows, :]] * (BLK // 128), axis=1)
            dl = jnp.concatenate([delta[rows, :]] * (BLK // 128), axis=1)
            p = e[kb, rows, :] * cf
            ds = (p * (dp[kb, rows, :] - dl)).astype(bf16)
            ds_out[i, rows, :] = ds
            from_scores = dot(qcat_t[:, rows], ds)
            from_values = dot(dlat_t[:, rows], p.astype(bf16))
            scores = from_scores if c == 0 else scores + from_scores
            values = from_values if c == 0 else values + from_values
        scores = scores * SCALE
        low = (scores[:LAT] + values).astype(bf16)
        high = scores[LAT:].astype(bf16)
        for q in range(4):
            r = (i, jnp.bitwise_xor(sc[1], q & 1), jnp.bitwise_xor(sc[2], q >> 1))
            at = place(sc[3], r)
            if q < 3:
                x_out[at] = low[q * COLS : (q + 1) * COLS]
            else:
                x_out[at, : LAT - 3 * COLS, :] = low[3 * COLS :]
                x_out[at, LAT - 3 * COLS :, :] = high


def second_first(sc, stat, qcat_t, dlat_t, e, dp, x_out, ds_out, coef, delta):
    m = stat[:, 0:8, :]
    best = jnp.max(m, axis=0)
    w = jnp.exp2(m - best[None])
    total = jnp.sum(w * stat[:, 8:16, :], axis=0)
    dtotal = jnp.sum(w * stat[:, 16:24, :], axis=0)
    cf = jnp.exp2(stat[sc[4], 0:8, :] - best) / total
    dl = dtotal / total
    for h in range(HEADS):
        rows = slice(h * ROWS, (h + 1) * ROWS)
        coef[rows, :] = jnp.broadcast_to(cf[h : h + 1], (128, 128)).T
        delta[rows, :] = jnp.broadcast_to(dl[h : h + 1], (128, 128)).T
    second(0, sc, coef, delta, qcat_t, dlat_t, e, dp, x_out, ds_out)


def run_second(sc, heads_in, qcat_t, dlat_t, e, dp, chain):
    first = len(heads_in) == 1
    outs = [((8, COLS, BLK), bf16), ((2, ALL, BLK), bf16)]
    if first:
        outs += [((ALL, 128), f32)] * 2
    return call(
        second_first if first else functools.partial(second, chain),
        "second_first" if first else "second",
        outs,
        (sc, *heads_in, qcat_t, dlat_t, e, dp),
        1,
        limit=LIMIT_TWO,
    )


def query_piece(chain, sc, ds, lat, *refs):
    total = None if len(refs) == 1 else refs[0][...]
    for i in range(2):
        kb = key_block(i, chain, sc)
        part = dot_nt(ds[i], lat[:, pl.ds(pl.multiple_of(kb * BLK, BLK), BLK)])
        total = part if total is None else total + part
    refs[-1][...] = total


def run_query_piece(chain, sc, ds, lat_t, *acc):
    kernel = functools.partial(query_piece, chain)
    return call(kernel, "query_piece", [((ALL, WIDE), f32)], (sc, ds, lat_t, *acc), 1)[0]


def query_last(acc, wuk, out, wide):
    for h in range(HEADS):
        rows = slice(h * ROWS, (h + 1) * ROWS)
        x = acc[rows, :LAT] * SCALE
        hi = x.astype(bf16)
        lo = (x - hi.astype(f32)).astype(bf16)
        wide[h, :, :NOPE] = dot_nt(hi, wuk[h]) + dot_nt(lo, wuk[h])
        wide[h, :, NOPE:] = acc[rows, LAT:] * SCALE
    for g in range(PEERS):
        out[g] = wide[:, g * 8 : (g + 1) * 8, :].reshape(HEADS * 8, NOPE + ROT).astype(bf16)


def run_query_last(acc, wuk):
    outs = [((PEERS, HEADS * 8, NOPE + ROT), bf16)]
    scratch = [pltpu.VMEM((HEADS, ROWS, NOPE + ROT), f32)]
    return call(query_last, "query_last", outs, (acc, wuk), 0, scratch)[0]


def halve(kept, got, *outs):
    n = kept.shape[0]
    for k in range(n):
        total = (kept[k].astype(f32) + got[k].astype(f32)).astype(bf16)
        outs[k * len(outs) // n][k % (n // len(outs))] = total


def run_halve(kept, got):
    n = kept.shape[0]
    outs = [((max(n // 2, 1), *kept.shape[1:]), bf16)] * min(n, 2)
    return call(halve, "halve", outs, (kept, got))


def join(own, got, out):
    n = own.shape[0]
    out[:n] = own[...]
    out[n:] = got[...]


def run_join(own, got):
    return call(join, "join", [((2 * own.shape[0], COLS, BLK), bf16)], (own, got))[0]


def settle(chain, sc, mine, mine_far, other, other_far, *refs):
    out, sem = refs[-2:]
    copies = []
    for near, far, half in ((mine, mine_far, sc[3]), (other, other_far, 1 - sc[3])):
        for i in range(8):
            b = (i >> 2 & 1, i >> 1 & 1, i & 1)
            r = [jnp.where(half == 0, b[d], b[(d + 2) % 3]) for d in range(3)]
            a = [jnp.bitwise_xor(sc[d], r[d]) for d in range(3)]
            rows = pl.ds(pl.multiple_of((a[2] * 2 + a[1]) * COLS, 16), COLS)
            lanes = pl.ds(pl.multiple_of((half * 4 + chain * 2 + a[0]) * BLK, BLK), BLK)
            block = near.at[i] if i < 4 else far.at[i - 4]
            copy = pltpu.make_async_copy(block, out.at[rows, lanes], sem.at[len(copies)])
            copy.start()
            copies.append(copy)
    for copy in copies:
        copy.wait()


def run_settle(chain, sc, pieces, *earlier):
    return pl.pallas_call(
        functools.partial(settle, chain),
        in_specs=[in_smem] + [in_vmem] * len(pieces) + [in_hbm] * len(earlier),
        out_specs=in_hbm,
        out_shape=jax.ShapeDtypeStruct((WIDE, KEYS), bf16),
        scratch_shapes=[pltpu.SemaphoreType.DMA((16,))],
        input_output_aliases={5: 0} if earlier else {},
        compiler_params=params(),
        name="settle",
    )(sc, *pieces, *earlier)


def cube_neighbour(k, d):
    y, rest = k >> 2, k & 3
    if d == 2:
        return k ^ 2
    gray = (y ^ (y >> 1)) ^ (1 << d)
    back = gray ^ (gray >> 1)
    return back * 4 + rest


def along(value, n):
    pairs = [(k, cube_neighbour(k, (n + (k & 1)) % 3)) for k in range(16)]
    return lax.ppermute(value, "head", pairs)


def to_sibling(value):
    return lax.ppermute(value, "head", [(k, k ^ 1) for k in range(16)])


def held(value):
    return pltpu.with_memory_space_constraint(value, pltpu.HBM)


def shards(queries, w_uk, w_uv, latent, out_grad, offsets):
    head = lax.axis_index("head").astype(jnp.int32)
    key = lax.axis_index("key").astype(jnp.int32)
    y = head >> 2
    gray = y ^ (y >> 1)
    core = head & 1
    sc_own = jnp.stack([gray & 1, gray >> 1, (head >> 1) & 1, core, key])
    sc_far = jnp.stack([gray & 1, gray >> 1, (head >> 1) & 1, 1 - core, key])
    lat_t = latent.T
    qt = jnp.transpose(queries, (1, 2, 0))
    og = out_grad.reshape(ALL, 128)
    e, dp, qcat_t, dlat_t, stat = run_pass_one(
        (key * KEYS)[None], *map(held, (offsets[None], qt, w_uk, w_uv, og, lat_t))
    )
    stat, sc_own, sc_far = lax.optimization_barrier((stat, sc_own, sc_far))
    stat = lax.all_to_all(stat, "key", 0, 0, tiled=True)
    turned = (qcat_t, dlat_t, e, dp)
    x_far, far_a, coef, delta = run_second(sc_far, (stat,), *turned, 0)
    came = to_sibling(x_far)
    x_own, own_a = run_second(sc_own, (coef, delta), *turned, 0)
    kept_a, send_a = run_halve(x_own, came)
    tie = lax.optimization_barrier
    sc_late, send_a = tie((sc_far, send_a))
    got_a = along(send_a, 0)
    x_far, far_b = run_second(sc_late, (coef, delta), *turned, 1)
    came = to_sibling(x_far)
    x_own, own_b = run_second(sc_own, (coef, delta), *turned, 1)
    kept_b, send_b = run_halve(x_own, came)
    got_b = along(send_b, 0)
    acc = run_query_piece(0, sc_far, far_a, lat_t)
    acc = run_query_piece(0, sc_own, own_a, lat_t, acc)
    got_a, acc = tie((got_a, acc))
    kept_a, send_a = run_halve(kept_a, got_a)
    kept_b, send_a, acc = tie((kept_b, send_a, acc))
    got_a = along(send_a, 1)
    acc = run_query_piece(1, sc_far, far_b, lat_t, acc)
    acc = run_query_piece(1, sc_own, own_b, lat_t, acc)
    got_b, acc = tie((got_b, acc))
    kept_b, send_b = run_halve(kept_b, got_b)
    kept_a, send_b, acc = tie((kept_a, send_b, acc))
    got_b = along(send_b, 1)
    dq = run_query_last(acc, w_uk)
    got_a, dq = tie((got_a, dq))
    kept_a, send_a = run_halve(kept_a, got_a)
    kept_b, send_a = tie((kept_b, send_a))
    got_a = along(send_a, 2)
    kept_b, send_b = run_halve(kept_b, got_b)
    kept_a, send_b = tie((kept_a, send_b))
    got_b = along(send_b, 2)
    (own_a,) = run_halve(kept_a, got_a)
    kept_b, own_a = tie((kept_b, own_a))
    got_a = along(own_a, 2)
    (own_b,) = run_halve(kept_b, got_b)
    own_a, own_b = tie((own_a, own_b))
    got_b = along(own_b, 2)
    got_a, dq = tie((got_a, dq))
    dq = lax.all_to_all(dq, "key", 0, 0, tiled=True)
    own_a = run_join(own_a, got_a)
    own_b, own_a = tie((own_b, own_a))
    got_a = along(own_a, 1)
    own_b = run_join(own_b, got_b)
    own_a, own_b = tie((own_a, own_b))
    got_b = along(own_b, 1)
    own_a = run_join(own_a, got_a)
    own_b, own_a = tie((own_b, own_a))
    far_a, near_a = along(own_a, 0), to_sibling(own_a)
    own_b = run_join(own_b, got_b)
    far_b, near_b = along(own_b, 0), to_sibling(own_b)
    pieces = [
        (own_a, far_a, near_a, to_sibling(far_a)),
        (own_b, far_b, near_b, to_sibling(far_b)),
    ]
    d_latent = run_settle(1, sc_own, pieces[1], run_settle(0, sc_own, pieces[0])).T

    dq = jnp.sum(dq.astype(f32), axis=0).astype(bf16)
    d_queries = jnp.transpose(dq.reshape(HEADS, 8, NOPE + ROT), (1, 0, 2))
    return (d_queries, d_latent)


def solution(mesh):
    return jax.shard_map(
        shards,
        mesh=mesh,
        in_specs=(
            P(None, "head", None),
            P("head", None, None),
            P("head", None, None),
            P("key", None),
            P(None, "head", None),
            P(),
        ),
        out_specs=(P("key", "head", None), P("key", None)),
        check_vma=False,
    )
```

```python
import functools
import math

import jax
import jax.numpy as jnp
from jax import lax
from jax.experimental import pallas as pl
from jax.experimental.pallas import tpu as pltpu
from jax.sharding import PartitionSpec as P

bf16 = jnp.bfloat16
f32 = jnp.float32
floor_score = -1e30
floor_top = -1e20

HEADS = 8
ROWS = 128
NOPE = 128
ROT = 64
LAT = 512
WIDE = LAT + ROT
KEYS = 2048
BLK = 256
NBLK = KEYS // BLK
ALL = HEADS * ROWS
PEERS = 16
COLS = WIDE // 4
SCALE = 1.0 / math.sqrt(NOPE + ROT)
SCALE2 = SCALE * math.log2(math.e)
VLIM = 14 * 1024 * 1024
LIMIT_ONE = 34 * 1024 * 1024
LIMIT_TWO = 28 * 1024 * 1024

NT = (((1,), (1,)), ((), ()))


def dot(a, b):
    return jnp.dot(a, b, preferred_element_type=f32)


def dot_nt(a, b):
    return lax.dot_general(a, b, NT, preferred_element_type=f32)


def params(limit=VLIM):
    return pltpu.CompilerParams(vmem_limit_bytes=limit)


in_vmem = pl.BlockSpec(memory_space=pltpu.VMEM)
in_hbm = pl.BlockSpec(memory_space=pltpu.HBM)
in_smem = pl.BlockSpec(memory_space=pltpu.SMEM)


def call(kernel, name, outs, args, scalars=0, scratch=(), limit=VLIM):
    return pl.pallas_call(
        kernel,
        in_specs=[in_smem] * scalars + [in_vmem] * (len(args) - scalars),
        out_specs=[in_vmem] * len(outs),
        out_shape=[jax.ShapeDtypeStruct(shape, kind) for shape, kind in outs],
        scratch_shapes=list(scratch),
        compiler_params=params(limit),
        name=name,
    )(*args)


CHUNK = 256


def pass_one(
    base, off, qt, wuk, wuv, og, lat,
    e_v, dp_v, qcat_t, dlat_t, stat,
    off_v, qt_v, wuk_v, wuv_v, og_v, lat_v, og_wide, qcat, dlat, top, tot, dsum, hide,
    sem_in, sem_lat,
):
    def load(source, target, sem):
        copy = pltpu.make_async_copy(source, target, sem)
        copy.start()
        return copy

    pairs = ((off, off_v), (qt, qt_v), (wuk, wuk_v))
    ahead = [load(*pair, sem_in.at[k]) for k, pair in enumerate(pairs)]
    blocks = [slice(j * BLK, (j + 1) * BLK) for j in range(NBLK)]
    lat_loads = [load(lat.at[:, c], lat_v.at[:, c], sem_lat.at[j]) for j, c in enumerate(blocks)]
    behind = [load(og, og_v, sem_in.at[3]), load(wuv, wuv_v, sem_in.at[4])]
    ahead[0].wait()
    bound = jnp.broadcast_to(off_v[...], (ROWS, ROWS)).T - base[0]
    bound = jnp.concatenate([bound] * (BLK // 128), axis=1)
    lane = lax.broadcasted_iota(jnp.int32, (ROWS, BLK), 1)
    top[...] = jnp.full((ALL, 128), floor_top, f32)
    tot[...] = jnp.zeros((ALL, 128), f32)
    dsum[...] = jnp.zeros((ALL, 128), f32)
    chunks = [slice(c * CHUNK, (c + 1) * CHUNK) for c in range(ALL // CHUNK)]
    heads = [slice(h * ROWS, (h + 1) * ROWS) for h in range(HEADS)]

    ahead[1].wait()
    ahead[2].wait()
    for h, rows in enumerate(heads):
        q = qt_v[h].T
        qcat[rows, :LAT] = dot(q[:, :NOPE], wuk_v[h]).astype(bf16)
        qcat[rows, LAT:] = q[:, NOPE:]
    for j, cols in enumerate(blocks):
        lat_loads[j].wait()
        hide[j] = jnp.where(lane + j * BLK <= bound, 0.0, floor_score)
        for rows in chunks:
            s = dot(qcat[rows, :], lat_v[:, cols])
            s = (s.reshape(CHUNK // ROWS, ROWS, BLK) + hide[j][None]).reshape(CHUNK, BLK)
            e_v[j, rows, :] = s
            best = top[rows, :]
            for k in range(BLK // 128):
                best = jnp.maximum(best, s[:, k * 128 : (k + 1) * 128])
            top[rows, :] = best
        rows = heads[j]
        for k in range(LAT // 128):
            lanes = slice(k * 128, (k + 1) * 128)
            qcat_t[lanes, rows] = qcat[rows, lanes].T
        qcat_t[LAT:, rows] = qcat[rows, LAT:].T
    for copy in behind:
        copy.wait()
    og_wide[...] = og_v[...].astype(f32)
    for h, rows in enumerate(heads):
        grad = og_wide[pl.ds(h, ROWS, stride=HEADS), :].astype(bf16)
        dlat[rows, :] = dot_nt(grad, wuv_v[h]).astype(bf16)
    top[...] = jnp.broadcast_to(jnp.max(top[...], axis=1, keepdims=True) * SCALE2, (ALL, 128))
    for j, cols in enumerate(blocks):
        for rows in chunks:
            dp = dot(dlat[rows, :], lat_v[:LAT, cols])
            dp_v[j, rows, :] = dp
            s = e_v[j, rows, :]
            m = top[rows, :]
            t, d = tot[rows, :], dsum[rows, :]
            for k in range(BLK // 128):
                lanes = slice(k * 128, (k + 1) * 128)
                e = jnp.exp2(s[:, lanes] * SCALE2 - m)
                e_v[j, rows, lanes] = e
                t = t + e
                d = d + e * dp[:, lanes]
            tot[rows, :] = t
            dsum[rows, :] = d
        rows = heads[j]
        for k in range(LAT // 128):
            lanes = slice(k * 128, (k + 1) * 128)
            dlat_t[lanes, rows] = dlat[rows, lanes].T
    near = lane[:, :128]
    for h, rows in enumerate(heads):
        t = jnp.sum(tot[rows, :], axis=1, keepdims=True)
        d = jnp.sum(dsum[rows, :], axis=1, keepdims=True)
        x = jnp.where(near == 0, top[rows, :], jnp.where(near == 1, t, d)).T
        for k in range(3):
            line = x[k : k + 1, :]
            for peer in range(PEERS):
                stat[peer, k * 8 + h : k * 8 + h + 1, :] = line


def run_pass_one(base, offsets, qt, wuk, wuv, og, lat_t):
    big = (NBLK, ALL, BLK)
    outs = [(big, f32), (big, f32), ((WIDE, ALL), bf16), ((LAT, ALL), bf16)]
    outs += [((PEERS, 24, 128), f32)]
    column = pltpu.VMEM((ALL, 128), f32)
    return pl.pallas_call(
        pass_one,
        in_specs=[in_smem] + [in_hbm] * 6,
        out_specs=[in_vmem] * 5,
        out_shape=[jax.ShapeDtypeStruct(shape, kind) for shape, kind in outs],
        scratch_shapes=[pltpu.VMEM(a.shape, a.dtype) for a in (offsets, qt, wuk, wuv, og, lat_t)]
        + [
            column,
            pltpu.VMEM((ALL, WIDE), bf16),
            pltpu.VMEM((ALL, LAT), bf16),
            column,
            column,
            column,
            pltpu.VMEM((NBLK, ROWS, BLK), f32),
            pltpu.SemaphoreType.DMA((5,)),
            pltpu.SemaphoreType.DMA((NBLK,)),
        ],
        compiler_params=params(LIMIT_ONE),
        name="pass_one",
    )(base, offsets, qt, wuk, wuv, og, lat_t)


def place(half, r):
    return jnp.where(half == 0, r[0] * 4 + r[1] * 2 + r[2], r[1] * 4 + r[2] * 2 + r[0])


def key_block(r0, chain, sc):
    return sc[3] * 4 + chain * 2 + jnp.bitwise_xor(sc[0], r0)


TALL = 512


def second(chain, sc, coef, delta, qcat_t, dlat_t, e, dp, x_out, ds_out):
    for i in range(2):
        kb = key_block(i, chain, sc)
        scores = values = None
        for c in range(ALL // TALL):
            rows = slice(c * TALL, (c + 1) * TALL)
            cf = jnp.concatenate([coef[rows, :]] * (BLK // 128), axis=1)
            dl = jnp.concatenate([delta[rows, :]] * (BLK // 128), axis=1)
            p = e[kb, rows, :] * cf
            ds = (p * (dp[kb, rows, :] - dl)).astype(bf16)
            ds_out[i, rows, :] = ds
            from_scores = dot(qcat_t[:, rows], ds)
            from_values = dot(dlat_t[:, rows], p.astype(bf16))
            scores = from_scores if c == 0 else scores + from_scores
            values = from_values if c == 0 else values + from_values
        scores = scores * SCALE
        low = (scores[:LAT] + values).astype(bf16)
        high = scores[LAT:].astype(bf16)
        for q in range(4):
            r = (i, jnp.bitwise_xor(sc[1], q & 1), jnp.bitwise_xor(sc[2], q >> 1))
            at = place(sc[3], r)
            if q < 3:
                x_out[at] = low[q * COLS : (q + 1) * COLS]
            else:
                x_out[at, : LAT - 3 * COLS, :] = low[3 * COLS :]
                x_out[at, LAT - 3 * COLS :, :] = high


def second_first(sc, stat, qcat_t, dlat_t, e, dp, x_out, ds_out, coef, delta):
    m = stat[:, 0:8, :]
    best = jnp.max(m, axis=0)
    w = jnp.exp2(m - best[None])
    total = jnp.sum(w * stat[:, 8:16, :], axis=0)
    dtotal = jnp.sum(w * stat[:, 16:24, :], axis=0)
    cf = jnp.exp2(stat[sc[4], 0:8, :] - best) / total
    dl = dtotal / total
    for h in range(HEADS):
        rows = slice(h * ROWS, (h + 1) * ROWS)
        coef[rows, :] = jnp.broadcast_to(cf[h : h + 1], (128, 128)).T
        delta[rows, :] = jnp.broadcast_to(dl[h : h + 1], (128, 128)).T
    second(0, sc, coef, delta, qcat_t, dlat_t, e, dp, x_out, ds_out)


def run_second(sc, heads_in, qcat_t, dlat_t, e, dp, chain):
    first = len(heads_in) == 1
    outs = [((8, COLS, BLK), bf16), ((2, ALL, BLK), bf16)]
    if first:
        outs += [((ALL, 128), f32)] * 2
    return call(
        second_first if first else functools.partial(second, chain),
        "second_first" if first else "second",
        outs,
        (sc, *heads_in, qcat_t, dlat_t, e, dp),
        1,
        limit=LIMIT_TWO,
    )


def query_piece(chain, sc, ds, lat, *refs):
    total = None if len(refs) == 1 else refs[0][...]
    for i in range(2):
        kb = key_block(i, chain, sc)
        part = dot_nt(ds[i], lat[:, pl.ds(pl.multiple_of(kb * BLK, BLK), BLK)])
        total = part if total is None else total + part
    refs[-1][...] = total


def run_query_piece(chain, sc, ds, lat_t, *acc):
    kernel = functools.partial(query_piece, chain)
    return call(kernel, "query_piece", [((ALL, WIDE), f32)], (sc, ds, lat_t, *acc), 1)[0]


def query_last(acc, wuk, out, wide):
    for h in range(HEADS):
        rows = slice(h * ROWS, (h + 1) * ROWS)
        x = acc[rows, :LAT] * SCALE
        hi = x.astype(bf16)
        lo = (x - hi.astype(f32)).astype(bf16)
        wide[h, :, :NOPE] = dot_nt(hi, wuk[h]) + dot_nt(lo, wuk[h])
        wide[h, :, NOPE:] = acc[rows, LAT:] * SCALE
    for g in range(PEERS):
        out[g] = wide[:, g * 8 : (g + 1) * 8, :].reshape(HEADS * 8, NOPE + ROT).astype(bf16)


def run_query_last(acc, wuk):
    outs = [((PEERS, HEADS * 8, NOPE + ROT), bf16)]
    scratch = [pltpu.VMEM((HEADS, ROWS, NOPE + ROT), f32)]
    return call(query_last, "query_last", outs, (acc, wuk), 0, scratch)[0]


def halve(kept, got, *outs):
    n = kept.shape[0]
    for k in range(n):
        total = (kept[k].astype(f32) + got[k].astype(f32)).astype(bf16)
        outs[k * len(outs) // n][k % (n // len(outs))] = total


def run_halve(kept, got):
    n = kept.shape[0]
    outs = [((max(n // 2, 1), *kept.shape[1:]), bf16)] * min(n, 2)
    return call(halve, "halve", outs, (kept, got))


def join(own, got, out):
    n = own.shape[0]
    out[:n] = own[...]
    out[n:] = got[...]


def run_join(own, got):
    return call(join, "join", [((2 * own.shape[0], COLS, BLK), bf16)], (own, got))[0]


def settle(parts, sc, *refs):
    out, sem = refs[-2:]
    copies = []
    for (chain, mine, far), piece in zip(parts, refs):
        half = sc[3] if mine else 1 - sc[3]
        for i in range(4):
            b = (far, i >> 1, i & 1)
            r = [jnp.where(half == 0, b[d], b[(d + 2) % 3]) for d in range(3)]
            a = [jnp.bitwise_xor(sc[d], r[d]) for d in range(3)]
            rows = pl.ds(pl.multiple_of((a[2] * 2 + a[1]) * COLS, 16), COLS)
            lanes = pl.ds(pl.multiple_of((half * 4 + chain * 2 + a[0]) * BLK, BLK), BLK)
            copy = pltpu.make_async_copy(piece.at[i], out.at[rows, lanes], sem.at[len(copies)])
            copy.start()
            copies.append(copy)
    for copy in copies:
        copy.wait()


def run_settle(parts, sc, pieces, *earlier):
    return pl.pallas_call(
        functools.partial(settle, parts),
        in_specs=[in_smem] + [in_vmem] * len(pieces) + [in_hbm] * len(earlier),
        out_specs=in_hbm,
        out_shape=jax.ShapeDtypeStruct((WIDE, KEYS), bf16),
        scratch_shapes=[pltpu.SemaphoreType.DMA((4 * len(pieces),))],
        input_output_aliases={1 + len(pieces): 0} if earlier else {},
        compiler_params=params(),
        name="settle",
    )(sc, *pieces, *earlier)


def cube_neighbour(k, d):
    y, rest = k >> 2, k & 3
    if d == 2:
        return k ^ 2
    gray = (y ^ (y >> 1)) ^ (1 << d)
    back = gray ^ (gray >> 1)
    return back * 4 + rest


def along(value, n):
    pairs = [(k, cube_neighbour(k, (n + (k & 1)) % 3)) for k in range(16)]
    return lax.ppermute(value, "head", pairs)


def to_sibling(value):
    return lax.ppermute(value, "head", [(k, k ^ 1) for k in range(16)])


def held(value):
    return pltpu.with_memory_space_constraint(value, pltpu.HBM)


def shards(queries, w_uk, w_uv, latent, out_grad, offsets):
    head = lax.axis_index("head").astype(jnp.int32)
    key = lax.axis_index("key").astype(jnp.int32)
    y = head >> 2
    gray = y ^ (y >> 1)
    core = head & 1
    sc_own = jnp.stack([gray & 1, gray >> 1, (head >> 1) & 1, core, key])
    sc_far = jnp.stack([gray & 1, gray >> 1, (head >> 1) & 1, 1 - core, key])
    lat_t = latent.T
    qt = jnp.transpose(queries, (1, 2, 0))
    og = out_grad.reshape(ALL, 128)
    e, dp, qcat_t, dlat_t, stat = run_pass_one(
        (key * KEYS)[None], *map(held, (offsets[None], qt, w_uk, w_uv, og, lat_t))
    )
    stat, sc_own, sc_far = lax.optimization_barrier((stat, sc_own, sc_far))
    stat = lax.all_to_all(stat, "key", 0, 0, tiled=True)
    turned = (qcat_t, dlat_t, e, dp)
    x_far, far_a, coef, delta = run_second(sc_far, (stat,), *turned, 0)
    came = to_sibling(x_far)
    x_own, own_a = run_second(sc_own, (coef, delta), *turned, 0)
    kept_a, send_a = run_halve(x_own, came)
    tie = lax.optimization_barrier
    sc_late, send_a = tie((sc_far, send_a))
    got_a = along(send_a, 0)
    x_far, far_b = run_second(sc_late, (coef, delta), *turned, 1)
    came = to_sibling(x_far)
    x_own, own_b = run_second(sc_own, (coef, delta), *turned, 1)
    kept_b, send_b = run_halve(x_own, came)
    got_b = along(send_b, 0)
    acc = run_query_piece(0, sc_far, far_a, lat_t)
    acc = run_query_piece(0, sc_own, own_a, lat_t, acc)
    got_a, acc = tie((got_a, acc))
    kept_a, send_a = run_halve(kept_a, got_a)
    kept_b, send_a, acc = tie((kept_b, send_a, acc))
    got_a = along(send_a, 1)
    acc = run_query_piece(1, sc_far, far_b, lat_t, acc)
    acc = run_query_piece(1, sc_own, own_b, lat_t, acc)
    got_b, acc = tie((got_b, acc))
    kept_b, send_b = run_halve(kept_b, got_b)
    kept_a, send_b, acc = tie((kept_a, send_b, acc))
    got_b = along(send_b, 1)
    dq = run_query_last(acc, w_uk)
    got_a, dq = tie((got_a, dq))
    kept_a, send_a = run_halve(kept_a, got_a)
    kept_b, send_a = tie((kept_b, send_a))
    got_a = along(send_a, 2)
    kept_b, send_b = run_halve(kept_b, got_b)
    kept_a, send_b = tie((kept_a, send_b))
    got_b = along(send_b, 2)
    (own_a,) = run_halve(kept_a, got_a)
    kept_b, own_a = tie((kept_b, own_a))
    got_a = along(own_a, 2)
    (own_b,) = run_halve(kept_b, got_b)
    own_a, own_b = tie((own_a, own_b))
    got_b = along(own_b, 2)
    got_a, dq = tie((got_a, dq))
    dq = lax.all_to_all(dq, "key", 0, 0, tiled=True)
    own_a = run_join(own_a, got_a)
    own_b, own_a = tie((own_b, own_a))
    got_a = along(own_a, 1)
    own_b = run_join(own_b, got_b)
    own_a, own_b = tie((own_a, own_b))
    got_b = along(own_b, 1)
    own_a = run_join(own_a, got_a)
    own_b, own_a = tie((own_b, own_a))
    far_a, near_a = along(own_a, 0), to_sibling(own_a)
    own_b = run_join(own_b, got_b)
    far_b, near_b = along(own_b, 0), to_sibling(own_b)
    near_parts = ((0, True, 0), (0, False, 0), (1, True, 0), (1, False, 0))
    out = run_settle(near_parts, sc_own, (own_a, near_a, own_b, near_b))
    other_a = to_sibling(far_a)
    far_b, out = tie((far_b, out))
    other_b = to_sibling(far_b)
    out = run_settle(((0, True, 1), (0, False, 1)), sc_own, (far_a, other_a), out)
    out = run_settle(((1, True, 1), (1, False, 1)), sc_own, (far_b, other_b), out)
    d_latent = out.T

    dq = jnp.sum(dq.astype(f32), axis=0).astype(bf16)
    d_queries = jnp.transpose(dq.reshape(HEADS, 8, NOPE + ROT), (1, 0, 2))
    return (d_queries, d_latent)


def solution(mesh):
    return jax.shard_map(
        shards,
        mesh=mesh,
        in_specs=(
            P(None, "head", None),
            P("head", None, None),
            P("head", None, None),
            P("key", None),
            P(None, "head", None),
            P(),
        ),
        out_specs=(P("key", "head", None), P("key", None)),
        check_vma=False,
    )
```

```python
import functools
import math

import jax
import jax.numpy as jnp
from jax import lax
from jax.experimental import pallas as pl
from jax.experimental.pallas import tpu as pltpu
from jax.sharding import PartitionSpec as P

bf16 = jnp.bfloat16
f32 = jnp.float32
floor_score = -1e30
floor_top = -1e20

HEADS = 8
ROWS = 128
NOPE = 128
ROT = 64
LAT = 512
WIDE = LAT + ROT
KEYS = 2048
BLK = 256
NBLK = KEYS // BLK
ALL = HEADS * ROWS
PEERS = 16
COLS = WIDE // 4
SCALE = 1.0 / math.sqrt(NOPE + ROT)
SCALE2 = SCALE * math.log2(math.e)
VLIM = 14 * 1024 * 1024
LIMIT_ONE = 34 * 1024 * 1024
LIMIT_TWO = 28 * 1024 * 1024

NT = (((1,), (1,)), ((), ()))


def dot(a, b):
    return jnp.dot(a, b, preferred_element_type=f32)


def dot_nt(a, b):
    return lax.dot_general(a, b, NT, preferred_element_type=f32)


def params(limit=VLIM):
    return pltpu.CompilerParams(vmem_limit_bytes=limit)


in_vmem = pl.BlockSpec(memory_space=pltpu.VMEM)
in_hbm = pl.BlockSpec(memory_space=pltpu.HBM)
in_smem = pl.BlockSpec(memory_space=pltpu.SMEM)


def call(kernel, name, outs, args, scalars=0, scratch=(), limit=VLIM):
    return pl.pallas_call(
        kernel,
        in_specs=[in_smem] * scalars + [in_vmem] * (len(args) - scalars),
        out_specs=[in_vmem] * len(outs),
        out_shape=[jax.ShapeDtypeStruct(shape, kind) for shape, kind in outs],
        scratch_shapes=list(scratch),
        compiler_params=params(limit),
        name=name,
    )(*args)


CHUNK = 256


def pass_one(
    base, off, qt, wuk, wuv, og, lat,
    e_v, dp_v, qcat_t, dlat_t, stat,
    off_v, qt_v, wuk_v, wuv_v, og_v, lat_v, og_wide, qcat, dlat, top, tot, dsum, hide, sem_in,
):
    pairs = ((off, off_v), (qt, qt_v), (wuk, wuk_v), (og, og_v), (wuv, wuv_v), (lat, lat_v))
    loads = [pltpu.make_async_copy(a, b, sem_in.at[k]) for k, (a, b) in enumerate(pairs)]
    for copy in loads:
        copy.start()
    loads[0].wait()
    bound = jnp.broadcast_to(off_v[...], (ROWS, ROWS)).T - base[0]
    bound = jnp.concatenate([bound] * (BLK // 128), axis=1)
    lane = lax.broadcasted_iota(jnp.int32, (ROWS, BLK), 1)
    top[...] = jnp.full((ALL, 128), floor_top, f32)
    tot[...] = jnp.zeros((ALL, 128), f32)
    dsum[...] = jnp.zeros((ALL, 128), f32)
    chunks = [slice(c * CHUNK, (c + 1) * CHUNK) for c in range(ALL // CHUNK)]
    heads = [slice(h * ROWS, (h + 1) * ROWS) for h in range(HEADS)]

    loads[1].wait()
    loads[2].wait()
    for h, rows in enumerate(heads):
        q = qt_v[h].T
        qcat[rows, :LAT] = dot(q[:, :NOPE], wuk_v[h]).astype(bf16)
        qcat[rows, LAT:] = q[:, NOPE:]
    loads[3].wait()
    loads[4].wait()
    og_wide[...] = og_v[...].astype(f32)
    for h, rows in enumerate(heads):
        grad = og_wide[pl.ds(h, ROWS, stride=HEADS), :].astype(bf16)
        dlat[rows, :] = dot_nt(grad, wuv_v[h]).astype(bf16)
    loads[5].wait()
    for rows in heads:
        for k in range(LAT // 128):
            lanes = slice(k * 128, (k + 1) * 128)
            qcat_t[lanes, rows] = qcat[rows, lanes].T
            dlat_t[lanes, rows] = dlat[rows, lanes].T
        qcat_t[LAT:, rows] = qcat[rows, LAT:].T

    def score(j, _):
        at = pl.multiple_of(j * BLK, BLK)
        hide[...] = jnp.where(lane + at <= bound, 0.0, floor_score)
        cols = lat_v[:, pl.ds(at, BLK)]
        for rows in chunks:
            s = dot(qcat[rows, :], cols)
            s = (s.reshape(CHUNK // ROWS, ROWS, BLK) + hide[...][None]).reshape(CHUNK, BLK)
            e_v[j, rows, :] = s
            best = top[rows, :]
            for k in range(BLK // 128):
                best = jnp.maximum(best, s[:, k * 128 : (k + 1) * 128])
            top[rows, :] = best
        return 0

    lax.fori_loop(0, NBLK, score, 0, unroll=NBLK)
    top[...] = jnp.broadcast_to(jnp.max(top[...], axis=1, keepdims=True) * SCALE2, (ALL, 128))

    def weigh(j, _):
        cols = lat_v[:LAT, pl.ds(pl.multiple_of(j * BLK, BLK), BLK)]
        for rows in chunks:
            dp = dot(dlat[rows, :], cols)
            dp_v[j, rows, :] = dp
            s = e_v[j, rows, :]
            m = top[rows, :]
            t, d = tot[rows, :], dsum[rows, :]
            for k in range(BLK // 128):
                lanes = slice(k * 128, (k + 1) * 128)
                e = jnp.exp2(s[:, lanes] * SCALE2 - m)
                e_v[j, rows, lanes] = e
                t = t + e
                d = d + e * dp[:, lanes]
            tot[rows, :] = t
            dsum[rows, :] = d
        return 0

    lax.fori_loop(0, NBLK, weigh, 0, unroll=NBLK)
    near = lane[:, :128]
    for h, rows in enumerate(heads):
        t = jnp.sum(tot[rows, :], axis=1, keepdims=True)
        d = jnp.sum(dsum[rows, :], axis=1, keepdims=True)
        x = jnp.where(near == 0, top[rows, :], jnp.where(near == 1, t, d)).T
        for k in range(3):
            line = x[k : k + 1, :]
            for peer in range(PEERS):
                stat[peer, k * 8 + h : k * 8 + h + 1, :] = line


def run_pass_one(base, offsets, qt, wuk, wuv, og, lat_t):
    big = (NBLK, ALL, BLK)
    outs = [(big, f32), (big, f32), ((WIDE, ALL), bf16), ((LAT, ALL), bf16)]
    outs += [((PEERS, 24, 128), f32)]
    column = pltpu.VMEM((ALL, 128), f32)
    return pl.pallas_call(
        pass_one,
        in_specs=[in_smem] + [in_hbm] * 6,
        out_specs=[in_vmem] * 5,
        out_shape=[jax.ShapeDtypeStruct(shape, kind) for shape, kind in outs],
        scratch_shapes=[pltpu.VMEM(a.shape, a.dtype) for a in (offsets, qt, wuk, wuv, og, lat_t)]
        + [
            column,
            pltpu.VMEM((ALL, WIDE), bf16),
            pltpu.VMEM((ALL, LAT), bf16),
            column,
            column,
            column,
            pltpu.VMEM((ROWS, BLK), f32),
            pltpu.SemaphoreType.DMA((6,)),
        ],
        compiler_params=params(LIMIT_ONE),
        name="pass_one",
    )(base, offsets, qt, wuk, wuv, og, lat_t)


def place(half, r):
    return jnp.where(half == 0, r[0] * 4 + r[1] * 2 + r[2], r[1] * 4 + r[2] * 2 + r[0])


def key_block(r0, chain, sc):
    return sc[3] * 4 + chain * 2 + jnp.bitwise_xor(sc[0], r0)


TALL = 512


def second(chain, sc, coef, delta, qcat_t, dlat_t, e, dp, x_out, ds_out):
    for i in range(2):
        kb = key_block(i, chain, sc)
        scores = values = None
        for c in range(ALL // TALL):
            rows = slice(c * TALL, (c + 1) * TALL)
            cf = jnp.concatenate([coef[rows, :]] * (BLK // 128), axis=1)
            dl = jnp.concatenate([delta[rows, :]] * (BLK // 128), axis=1)
            p = e[kb, rows, :] * cf
            ds = (p * (dp[kb, rows, :] - dl)).astype(bf16)
            ds_out[i, rows, :] = ds
            from_scores = dot(qcat_t[:, rows], ds)
            from_values = dot(dlat_t[:, rows], p.astype(bf16))
            scores = from_scores if c == 0 else scores + from_scores
            values = from_values if c == 0 else values + from_values
        scores = scores * SCALE
        low = (scores[:LAT] + values).astype(bf16)
        high = scores[LAT:].astype(bf16)
        for q in range(4):
            r = (i, jnp.bitwise_xor(sc[1], q & 1), jnp.bitwise_xor(sc[2], q >> 1))
            at = place(sc[3], r)
            if q < 3:
                x_out[at] = low[q * COLS : (q + 1) * COLS]
            else:
                x_out[at, : LAT - 3 * COLS, :] = low[3 * COLS :]
                x_out[at, LAT - 3 * COLS :, :] = high


def second_first(sc, stat, qcat_t, dlat_t, e, dp, x_out, ds_out, coef, delta):
    m = stat[:, 0:8, :]
    best = jnp.max(m, axis=0)
    w = jnp.exp2(m - best[None])
    total = jnp.sum(w * stat[:, 8:16, :], axis=0)
    dtotal = jnp.sum(w * stat[:, 16:24, :], axis=0)
    cf = jnp.exp2(stat[sc[4], 0:8, :] - best) / total
    dl = dtotal / total
    for h in range(HEADS):
        rows = slice(h * ROWS, (h + 1) * ROWS)
        coef[rows, :] = jnp.broadcast_to(cf[h : h + 1], (128, 128)).T
        delta[rows, :] = jnp.broadcast_to(dl[h : h + 1], (128, 128)).T
    second(0, sc, coef, delta, qcat_t, dlat_t, e, dp, x_out, ds_out)


def run_second(sc, heads_in, qcat_t, dlat_t, e, dp, chain):
    first = len(heads_in) == 1
    outs = [((8, COLS, BLK), bf16), ((2, ALL, BLK), bf16)]
    if first:
        outs += [((ALL, 128), f32)] * 2
    return call(
        second_first if first else functools.partial(second, chain),
        "second_first" if first else "second",
        outs,
        (sc, *heads_in, qcat_t, dlat_t, e, dp),
        1,
        limit=LIMIT_TWO,
    )


def query_piece(chain, sc, ds, lat, *refs):
    total = None if len(refs) == 1 else refs[0][...]
    for i in range(2):
        kb = key_block(i, chain, sc)
        part = dot_nt(ds[i], lat[:, pl.ds(pl.multiple_of(kb * BLK, BLK), BLK)])
        total = part if total is None else total + part
    refs[-1][...] = total


def run_query_piece(chain, sc, ds, lat_t, *acc):
    kernel = functools.partial(query_piece, chain)
    return call(kernel, "query_piece", [((ALL, WIDE), f32)], (sc, ds, lat_t, *acc), 1)[0]


def query_last(acc, wuk, out, wide):
    for h in range(HEADS):
        rows = slice(h * ROWS, (h + 1) * ROWS)
        x = acc[rows, :LAT] * SCALE
        hi = x.astype(bf16)
        lo = (x - hi.astype(f32)).astype(bf16)
        wide[h, :, :NOPE] = dot_nt(hi, wuk[h]) + dot_nt(lo, wuk[h])
        wide[h, :, NOPE:] = acc[rows, LAT:] * SCALE
    for g in range(PEERS):
        out[g] = wide[:, g * 8 : (g + 1) * 8, :].reshape(HEADS * 8, NOPE + ROT).astype(bf16)


def run_query_last(acc, wuk):
    outs = [((PEERS, HEADS * 8, NOPE + ROT), bf16)]
    scratch = [pltpu.VMEM((HEADS, ROWS, NOPE + ROT), f32)]
    return call(query_last, "query_last", outs, (acc, wuk), 0, scratch)[0]


def halve(kept, got, *outs):
    n = kept.shape[0]
    for k in range(n):
        total = (kept[k].astype(f32) + got[k].astype(f32)).astype(bf16)
        outs[k * len(outs) // n][k % (n // len(outs))] = total


def run_halve(kept, got):
    n = kept.shape[0]
    outs = [((max(n // 2, 1), *kept.shape[1:]), bf16)] * min(n, 2)
    return call(halve, "halve", outs, (kept, got))


def join(own, got, out):
    n = own.shape[0]
    out[:n] = own[...]
    out[n:] = got[...]


def run_join(own, got):
    return call(join, "join", [((2 * own.shape[0], COLS, BLK), bf16)], (own, got))[0]


def settle(parts, sc, *refs):
    out, sem = refs[-2:]
    copies = []
    for (chain, mine, far), piece in zip(parts, refs):
        half = sc[3] if mine else 1 - sc[3]
        for i in range(4):
            b = (far, i >> 1, i & 1)
            r = [jnp.where(half == 0, b[d], b[(d + 2) % 3]) for d in range(3)]
            a = [jnp.bitwise_xor(sc[d], r[d]) for d in range(3)]
            rows = pl.ds(pl.multiple_of((a[2] * 2 + a[1]) * COLS, 16), COLS)
            lanes = pl.ds(pl.multiple_of((half * 4 + chain * 2 + a[0]) * BLK, BLK), BLK)
            copy = pltpu.make_async_copy(piece.at[i], out.at[rows, lanes], sem.at[len(copies)])
            copy.start()
            copies.append(copy)
    for copy in copies:
        copy.wait()


def run_settle(parts, sc, pieces, *earlier):
    return pl.pallas_call(
        functools.partial(settle, parts),
        in_specs=[in_smem] + [in_vmem] * len(pieces) + [in_hbm] * len(earlier),
        out_specs=in_hbm,
        out_shape=jax.ShapeDtypeStruct((WIDE, KEYS), bf16),
        scratch_shapes=[pltpu.SemaphoreType.DMA((4 * len(pieces),))],
        input_output_aliases={1 + len(pieces): 0} if earlier else {},
        compiler_params=params(),
        name="settle",
    )(sc, *pieces, *earlier)


def cube_neighbour(k, d):
    y, rest = k >> 2, k & 3
    if d == 2:
        return k ^ 2
    gray = (y ^ (y >> 1)) ^ (1 << d)
    back = gray ^ (gray >> 1)
    return back * 4 + rest


def along(value, n):
    pairs = [(k, cube_neighbour(k, (n + (k & 1)) % 3)) for k in range(16)]
    return lax.ppermute(value, "head", pairs)


def to_sibling(value):
    return lax.ppermute(value, "head", [(k, k ^ 1) for k in range(16)])


def held(value):
    return pltpu.with_memory_space_constraint(value, pltpu.HBM)


def shards(queries, w_uk, w_uv, latent, out_grad, offsets):
    head = lax.axis_index("head").astype(jnp.int32)
    key = lax.axis_index("key").astype(jnp.int32)
    y = head >> 2
    gray = y ^ (y >> 1)
    core = head & 1
    sc_own = jnp.stack([gray & 1, gray >> 1, (head >> 1) & 1, core, key])
    sc_far = jnp.stack([gray & 1, gray >> 1, (head >> 1) & 1, 1 - core, key])
    lat_t = latent.T
    qt = jnp.transpose(queries, (1, 2, 0))
    og = out_grad.reshape(ALL, 128)
    e, dp, qcat_t, dlat_t, stat = run_pass_one(
        (key * KEYS)[None], *map(held, (offsets[None], qt, w_uk, w_uv, og, lat_t))
    )
    stat, sc_own, sc_far = lax.optimization_barrier((stat, sc_own, sc_far))
    stat = lax.all_to_all(stat, "key", 0, 0, tiled=True)
    turned = (qcat_t, dlat_t, e, dp)
    x_far, far_a, coef, delta = run_second(sc_far, (stat,), *turned, 0)
    came = to_sibling(x_far)
    x_own, own_a = run_second(sc_own, (coef, delta), *turned, 0)
    kept_a, send_a = run_halve(x_own, came)
    tie = lax.optimization_barrier
    sc_late, send_a = tie((sc_far, send_a))
    got_a = along(send_a, 0)
    x_far, far_b = run_second(sc_late, (coef, delta), *turned, 1)
    came = to_sibling(x_far)
    x_own, own_b = run_second(sc_own, (coef, delta), *turned, 1)
    kept_b, send_b = run_halve(x_own, came)
    got_b = along(send_b, 0)
    acc = run_query_piece(0, sc_far, far_a, lat_t)
    acc = run_query_piece(0, sc_own, own_a, lat_t, acc)
    got_a, acc = tie((got_a, acc))
    kept_a, send_a = run_halve(kept_a, got_a)
    kept_b, send_a, acc = tie((kept_b, send_a, acc))
    got_a = along(send_a, 1)
    acc = run_query_piece(1, sc_far, far_b, lat_t, acc)
    acc = run_query_piece(1, sc_own, own_b, lat_t, acc)
    got_b, acc = tie((got_b, acc))
    kept_b, send_b = run_halve(kept_b, got_b)
    kept_a, send_b, acc = tie((kept_a, send_b, acc))
    got_b = along(send_b, 1)
    dq = run_query_last(acc, w_uk)
    got_a, dq = tie((got_a, dq))
    kept_a, send_a = run_halve(kept_a, got_a)
    kept_b, send_a = tie((kept_b, send_a))
    got_a = along(send_a, 2)
    kept_b, send_b = run_halve(kept_b, got_b)
    kept_a, send_b = tie((kept_a, send_b))
    got_b = along(send_b, 2)
    (own_a,) = run_halve(kept_a, got_a)
    kept_b, own_a = tie((kept_b, own_a))
    got_a = along(own_a, 2)
    (own_b,) = run_halve(kept_b, got_b)
    own_b, dq = tie((own_b, dq))
    dq = lax.all_to_all(dq, "key", 0, 0, tiled=True)
    own_a, own_b = tie((own_a, own_b))
    got_b = along(own_b, 2)
    own_a = run_join(own_a, got_a)
    own_b, own_a = tie((own_b, own_a))
    got_a = along(own_a, 1)
    own_b = run_join(own_b, got_b)
    own_a, own_b = tie((own_a, own_b))
    got_b = along(own_b, 1)
    own_a = run_join(own_a, got_a)
    own_b, own_a = tie((own_b, own_a))
    far_a, near_a = along(own_a, 0), to_sibling(own_a)
    own_b = run_join(own_b, got_b)
    far_b, near_b = along(own_b, 0), to_sibling(own_b)
    near_parts = ((0, True, 0), (0, False, 0), (1, True, 0), (1, False, 0))
    out = run_settle(near_parts, sc_own, (own_a, near_a, own_b, near_b))
    other_a = to_sibling(far_a)
    far_b, out = tie((far_b, out))
    other_b = to_sibling(far_b)
    far_parts = ((0, True, 1), (0, False, 1), (1, True, 1), (1, False, 1))
    out = run_settle(far_parts, sc_own, (far_a, other_a, far_b, other_b), out)
    d_latent = out.T

    dq = jnp.sum(dq.astype(f32), axis=0).astype(bf16)
    d_queries = jnp.transpose(dq.reshape(HEADS, 8, NOPE + ROT), (1, 0, 2))
    return (d_queries, d_latent)


def solution(mesh):
    return jax.shard_map(
        shards,
        mesh=mesh,
        in_specs=(
            P(None, "head", None),
            P("head", None, None),
            P("head", None, None),
            P("key", None),
            P(None, "head", None),
            P(),
        ),
        out_specs=(P("key", "head", None), P("key", None)),
        check_vma=False,
    )
```

```python
import functools
import math

import jax
import jax.numpy as jnp
from jax import lax
from jax.experimental import pallas as pl
from jax.experimental.pallas import tpu as pltpu
from jax.sharding import PartitionSpec as P

bf16 = jnp.bfloat16
f32 = jnp.float32
floor_score = -1e30
floor_top = -1e20

HEADS = 8
ROWS = 128
NOPE = 128
ROT = 64
LAT = 512
WIDE = LAT + ROT
KEYS = 2048
BLK = 256
NBLK = KEYS // BLK
ALL = HEADS * ROWS
PEERS = 16
COLS = WIDE // 4
SCALE = 1.0 / math.sqrt(NOPE + ROT)
SCALE2 = SCALE * math.log2(math.e)
VLIM = 14 * 1024 * 1024
LIMIT_ONE = 34 * 1024 * 1024
LIMIT_TWO = 28 * 1024 * 1024

NT = (((1,), (1,)), ((), ()))


def dot(a, b):
    return jnp.dot(a, b, preferred_element_type=f32)


def dot_nt(a, b):
    return lax.dot_general(a, b, NT, preferred_element_type=f32)


def params(limit=VLIM):
    return pltpu.CompilerParams(vmem_limit_bytes=limit)


in_vmem = pl.BlockSpec(memory_space=pltpu.VMEM)
in_hbm = pl.BlockSpec(memory_space=pltpu.HBM)
in_smem = pl.BlockSpec(memory_space=pltpu.SMEM)


def call(kernel, name, outs, args, scalars=0, scratch=(), limit=VLIM):
    return pl.pallas_call(
        kernel,
        in_specs=[in_smem] * scalars + [in_vmem] * (len(args) - scalars),
        out_specs=[in_vmem] * len(outs),
        out_shape=[jax.ShapeDtypeStruct(shape, kind) for shape, kind in outs],
        scratch_shapes=list(scratch),
        compiler_params=params(limit),
        name=name,
    )(*args)


CHUNK = 256


def pass_one(
    base, off, qt, wuk, wuv, og, lat,
    e_v, dp_v, qcat_t, dlat_t, stat,
    off_v, qt_v, wuk_v, wuv_v, og_v, lat_v, og_wide, qcat, dlat, top, tot, dsum, hide, sem_in,
):
    pairs = ((off, off_v), (qt, qt_v), (wuk, wuk_v), (og, og_v), (wuv, wuv_v), (lat, lat_v))
    loads = [pltpu.make_async_copy(a, b, sem_in.at[k]) for k, (a, b) in enumerate(pairs)]
    for copy in loads:
        copy.start()
    loads[0].wait()
    bound = jnp.broadcast_to(off_v[...], (ROWS, ROWS)).T - base[0]
    bound = jnp.concatenate([bound] * (BLK // 128), axis=1)
    lane = lax.broadcasted_iota(jnp.int32, (ROWS, BLK), 1)
    top[...] = jnp.full((ALL, 128), floor_top, f32)
    tot[...] = jnp.zeros((ALL, 128), f32)
    dsum[...] = jnp.zeros((ALL, 128), f32)
    chunks = [slice(c * CHUNK, (c + 1) * CHUNK) for c in range(ALL // CHUNK)]
    heads = [slice(h * ROWS, (h + 1) * ROWS) for h in range(HEADS)]

    loads[1].wait()
    loads[2].wait()
    for h, rows in enumerate(heads):
        q = qt_v[h].T
        qcat[rows, :LAT] = dot(q[:, :NOPE], wuk_v[h]).astype(bf16)
        qcat[rows, LAT:] = q[:, NOPE:]
    loads[3].wait()
    loads[4].wait()
    og_wide[...] = og_v[...].astype(f32)
    for h, rows in enumerate(heads):
        grad = og_wide[pl.ds(h, ROWS, stride=HEADS), :].astype(bf16)
        dlat[rows, :] = dot_nt(grad, wuv_v[h]).astype(bf16)
    loads[5].wait()
    for rows in heads:
        for k in range(LAT // 128):
            lanes = slice(k * 128, (k + 1) * 128)
            qcat_t[lanes, rows] = qcat[rows, lanes].T
            dlat_t[lanes, rows] = dlat[rows, lanes].T
        qcat_t[LAT:, rows] = qcat[rows, LAT:].T

    def score(j, _):
        at = pl.multiple_of(j * BLK, BLK)
        hide[...] = jnp.where(lane + at <= bound, 0.0, floor_score)
        cols = lat_v[:, pl.ds(at, BLK)]
        for rows in chunks:
            s = dot(qcat[rows, :], cols)
            s = (s.reshape(CHUNK // ROWS, ROWS, BLK) + hide[...][None]).reshape(CHUNK, BLK)
            e_v[j, rows, :] = s
            best = top[rows, :]
            for k in range(BLK // 128):
                best = jnp.maximum(best, s[:, k * 128 : (k + 1) * 128])
            top[rows, :] = best
        return 0

    lax.fori_loop(0, NBLK, score, 0, unroll=NBLK)
    top[...] = jnp.broadcast_to(jnp.max(top[...], axis=1, keepdims=True) * SCALE2, (ALL, 128))

    def weigh(j, _):
        cols = lat_v[:LAT, pl.ds(pl.multiple_of(j * BLK, BLK), BLK)]
        for rows in chunks:
            dp = dot(dlat[rows, :], cols)
            dp_v[j, rows, :] = dp
            s = e_v[j, rows, :]
            m = top[rows, :]
            t, d = tot[rows, :], dsum[rows, :]
            for k in range(BLK // 128):
                lanes = slice(k * 128, (k + 1) * 128)
                e = jnp.exp2(s[:, lanes] * SCALE2 - m)
                e_v[j, rows, lanes] = e
                t = t + e
                d = d + e * dp[:, lanes]
            tot[rows, :] = t
            dsum[rows, :] = d
        return 0

    lax.fori_loop(0, NBLK, weigh, 0, unroll=NBLK)
    near = lane[:, :128]
    for h, rows in enumerate(heads):
        t = jnp.sum(tot[rows, :], axis=1, keepdims=True)
        d = jnp.sum(dsum[rows, :], axis=1, keepdims=True)
        x = jnp.where(near == 0, top[rows, :], jnp.where(near == 1, t, d)).T
        for k in range(3):
            line = x[k : k + 1, :]
            for peer in range(PEERS):
                stat[peer, k * 8 + h : k * 8 + h + 1, :] = line


def run_pass_one(base, offsets, qt, wuk, wuv, og, lat_t):
    big = (NBLK, ALL, BLK)
    outs = [(big, f32), (big, f32), ((WIDE, ALL), bf16), ((LAT, ALL), bf16)]
    outs += [((PEERS, 24, 128), f32)]
    column = pltpu.VMEM((ALL, 128), f32)
    return pl.pallas_call(
        pass_one,
        in_specs=[in_smem] + [in_hbm] * 6,
        out_specs=[in_vmem] * 5,
        out_shape=[jax.ShapeDtypeStruct(shape, kind) for shape, kind in outs],
        scratch_shapes=[pltpu.VMEM(a.shape, a.dtype) for a in (offsets, qt, wuk, wuv, og, lat_t)]
        + [
            column,
            pltpu.VMEM((ALL, WIDE), bf16),
            pltpu.VMEM((ALL, LAT), bf16),
            column,
            column,
            column,
            pltpu.VMEM((ROWS, BLK), f32),
            pltpu.SemaphoreType.DMA((6,)),
        ],
        compiler_params=params(LIMIT_ONE),
        name="pass_one",
    )(base, offsets, qt, wuk, wuv, og, lat_t)


def place(half, r):
    return jnp.where(half == 0, r[0] * 4 + r[1] * 2 + r[2], r[1] * 4 + r[2] * 2 + r[0])


def key_block(r0, chain, sc):
    return sc[3] * 4 + chain * 2 + jnp.bitwise_xor(sc[0], r0)


TALL = 512


def second(chain, sc, coef, delta, qcat_t, dlat_t, e, dp, x_out, ds_out):
    for i in range(2):
        kb = key_block(i, chain, sc)
        scores = values = None
        for c in range(ALL // TALL):
            rows = slice(c * TALL, (c + 1) * TALL)
            cf = jnp.concatenate([coef[rows, :]] * (BLK // 128), axis=1)
            dl = jnp.concatenate([delta[rows, :]] * (BLK // 128), axis=1)
            p = e[kb, rows, :] * cf
            ds = (p * (dp[kb, rows, :] - dl)).astype(bf16)
            ds_out[i, rows, :] = ds
            from_scores = dot(qcat_t[:, rows], ds)
            from_values = dot(dlat_t[:, rows], p.astype(bf16))
            scores = from_scores if c == 0 else scores + from_scores
            values = from_values if c == 0 else values + from_values
        scores = scores * SCALE
        low = (scores[:LAT] + values).astype(bf16)
        high = scores[LAT:].astype(bf16)
        for q in range(4):
            r = (i, jnp.bitwise_xor(sc[1], q & 1), jnp.bitwise_xor(sc[2], q >> 1))
            at = place(sc[3], r)
            if q < 3:
                x_out[at] = low[q * COLS : (q + 1) * COLS]
            else:
                x_out[at, : LAT - 3 * COLS, :] = low[3 * COLS :]
                x_out[at, LAT - 3 * COLS :, :] = high


def second_first(sc, stat, qcat_t, dlat_t, e, dp, x_out, ds_out, coef, delta):
    m = stat[:, 0:8, :]
    best = jnp.max(m, axis=0)
    w = jnp.exp2(m - best[None])
    total = jnp.sum(w * stat[:, 8:16, :], axis=0)
    dtotal = jnp.sum(w * stat[:, 16:24, :], axis=0)
    cf = jnp.exp2(stat[sc[4], 0:8, :] - best) / total
    dl = dtotal / total
    for h in range(HEADS):
        rows = slice(h * ROWS, (h + 1) * ROWS)
        coef[rows, :] = jnp.broadcast_to(cf[h : h + 1], (128, 128)).T
        delta[rows, :] = jnp.broadcast_to(dl[h : h + 1], (128, 128)).T
    second(0, sc, coef, delta, qcat_t, dlat_t, e, dp, x_out, ds_out)


def run_second(sc, heads_in, qcat_t, dlat_t, e, dp, chain):
    first = len(heads_in) == 1
    outs = [((8, COLS, BLK), bf16), ((2, ALL, BLK), bf16)]
    if first:
        outs += [((ALL, 128), f32)] * 2
    return call(
        second_first if first else functools.partial(second, chain),
        "second_first" if first else "second",
        outs,
        (sc, *heads_in, qcat_t, dlat_t, e, dp),
        1,
        limit=LIMIT_TWO,
    )


def query_piece(chain, sc, ds, lat, *refs):
    total = None if len(refs) == 1 else refs[0][...]
    for i in range(2):
        kb = key_block(i, chain, sc)
        part = dot_nt(ds[i], lat[:, pl.ds(pl.multiple_of(kb * BLK, BLK), BLK)])
        total = part if total is None else total + part
    refs[-1][...] = total


def run_query_piece(chain, sc, ds, lat_t, *acc):
    kernel = functools.partial(query_piece, chain)
    return call(kernel, "query_piece", [((ALL, WIDE), f32)], (sc, ds, lat_t, *acc), 1)[0]


def query_last(acc, wuk, out, wide):
    for h in range(HEADS):
        rows = slice(h * ROWS, (h + 1) * ROWS)
        x = acc[rows, :LAT] * SCALE
        hi = x.astype(bf16)
        lo = (x - hi.astype(f32)).astype(bf16)
        wide[h, :, :NOPE] = dot_nt(hi, wuk[h]) + dot_nt(lo, wuk[h])
        wide[h, :, NOPE:] = acc[rows, LAT:] * SCALE
    for g in range(PEERS):
        out[g] = wide[:, g * 8 : (g + 1) * 8, :].reshape(HEADS * 8, NOPE + ROT).astype(bf16)


def run_query_last(acc, wuk):
    outs = [((PEERS, HEADS * 8, NOPE + ROT), bf16)]
    scratch = [pltpu.VMEM((HEADS, ROWS, NOPE + ROT), f32)]
    return call(query_last, "query_last", outs, (acc, wuk), 0, scratch)[0]


def halve(kept, got, *outs):
    n = kept.shape[0]
    for k in range(n):
        total = (kept[k].astype(f32) + got[k].astype(f32)).astype(bf16)
        outs[k * len(outs) // n][k % (n // len(outs))] = total


def run_halve(kept, got):
    n = kept.shape[0]
    outs = [((max(n // 2, 1), *kept.shape[1:]), bf16)] * min(n, 2)
    return call(halve, "halve", outs, (kept, got))


def join(own, got, out):
    n = own.shape[0]
    out[:n] = own[...]
    out[n:] = got[...]


def run_join(own, got):
    return call(join, "join", [((2 * own.shape[0], COLS, BLK), bf16)], (own, got))[0]


def settle_start(parts, sc, pieces, out, sem):
    copies = []
    for (chain, mine, far), piece in zip(parts, pieces):
        half = sc[3] if mine else 1 - sc[3]
        for i in range(4):
            b = (far, i >> 1, i & 1)
            r = [jnp.where(half == 0, b[d], b[(d + 2) % 3]) for d in range(3)]
            a = [jnp.bitwise_xor(sc[d], r[d]) for d in range(3)]
            rows = pl.ds(pl.multiple_of((a[2] * 2 + a[1]) * COLS, 16), COLS)
            lanes = pl.ds(pl.multiple_of((half * 4 + chain * 2 + a[0]) * BLK, BLK), BLK)
            copy = pltpu.make_async_copy(piece.at[i], out.at[rows, lanes], sem.at[len(copies)])
            copy.start()
            copies.append(copy)
    return copies


def settle_near(parts, sc, *refs):
    for copy in settle_start(parts, sc, refs[:4], *refs[4:]):
        copy.wait()


def settle_far(parts, sc, a, b, c, d, dq, earlier, out, dq_out, sem, low, high):
    copies = settle_start(parts, sc, (a, b, c, d), out, sem)
    total = dq[0].astype(f32)
    for g in range(1, PEERS):
        total = total + dq[g].astype(f32)
    low[...] = total[:, :NOPE]
    high[:, :ROT] = total[:, NOPE:]
    for r in range(8):
        rows = pl.ds(r, HEADS, stride=8)
        dq_out[r, :, :NOPE] = low[rows, :].astype(bf16)
        dq_out[r, :, NOPE:] = high[rows, :][:, :ROT].astype(bf16)
    for copy in copies:
        copy.wait()


def run_settle_near(parts, sc, pieces):
    return pl.pallas_call(
        functools.partial(settle_near, parts),
        in_specs=[in_smem] + [in_vmem] * 4,
        out_specs=in_hbm,
        out_shape=jax.ShapeDtypeStruct((WIDE, KEYS), bf16),
        scratch_shapes=[pltpu.SemaphoreType.DMA((16,))],
        compiler_params=params(),
        name="settle_near",
    )(sc, *pieces)


def run_settle_far(parts, sc, pieces, dq, earlier):
    return pl.pallas_call(
        functools.partial(settle_far, parts),
        in_specs=[in_smem] + [in_vmem] * 5 + [in_hbm],
        out_specs=[in_hbm, in_vmem],
        out_shape=[
            jax.ShapeDtypeStruct((WIDE, KEYS), bf16),
            jax.ShapeDtypeStruct((8, HEADS, NOPE + ROT), bf16),
        ],
        scratch_shapes=[
            pltpu.SemaphoreType.DMA((16,)),
            pltpu.VMEM((HEADS * 8, 128), f32),
            pltpu.VMEM((HEADS * 8, 128), f32),
        ],
        input_output_aliases={6: 0},
        compiler_params=params(),
        name="settle_far",
    )(sc, *pieces, dq, earlier)


def cube_neighbour(k, d):
    y, rest = k >> 2, k & 3
    if d == 2:
        return k ^ 2
    gray = (y ^ (y >> 1)) ^ (1 << d)
    back = gray ^ (gray >> 1)
    return back * 4 + rest


def along(value, n):
    pairs = [(k, cube_neighbour(k, (n + (k & 1)) % 3)) for k in range(16)]
    return lax.ppermute(value, "head", pairs)


def to_sibling(value):
    return lax.ppermute(value, "head", [(k, k ^ 1) for k in range(16)])


def held(value):
    return pltpu.with_memory_space_constraint(value, pltpu.HBM)


def shards(queries, w_uk, w_uv, latent, out_grad, offsets):
    head = lax.axis_index("head").astype(jnp.int32)
    key = lax.axis_index("key").astype(jnp.int32)
    y = head >> 2
    gray = y ^ (y >> 1)
    core = head & 1
    sc_own = jnp.stack([gray & 1, gray >> 1, (head >> 1) & 1, core, key])
    sc_far = jnp.stack([gray & 1, gray >> 1, (head >> 1) & 1, 1 - core, key])
    lat_t = latent.T
    qt = jnp.transpose(queries, (1, 2, 0))
    og = out_grad.reshape(ALL, 128)
    e, dp, qcat_t, dlat_t, stat = run_pass_one(
        (key * KEYS)[None], *map(held, (offsets[None], qt, w_uk, w_uv, og, lat_t))
    )
    stat, sc_own, sc_far = lax.optimization_barrier((stat, sc_own, sc_far))
    stat = lax.all_to_all(stat, "key", 0, 0, tiled=True)
    turned = (qcat_t, dlat_t, e, dp)
    x_far, far_a, coef, delta = run_second(sc_far, (stat,), *turned, 0)
    came = to_sibling(x_far)
    x_own, own_a = run_second(sc_own, (coef, delta), *turned, 0)
    kept_a, send_a = run_halve(x_own, came)
    tie = lax.optimization_barrier
    sc_late, send_a = tie((sc_far, send_a))
    got_a = along(send_a, 0)
    x_far, far_b = run_second(sc_late, (coef, delta), *turned, 1)
    came = to_sibling(x_far)
    x_own, own_b = run_second(sc_own, (coef, delta), *turned, 1)
    kept_b, send_b = run_halve(x_own, came)
    got_b = along(send_b, 0)
    acc = run_query_piece(0, sc_far, far_a, lat_t)
    acc = run_query_piece(0, sc_own, own_a, lat_t, acc)
    got_a, acc = tie((got_a, acc))
    kept_a, send_a = run_halve(kept_a, got_a)
    kept_b, send_a, acc = tie((kept_b, send_a, acc))
    got_a = along(send_a, 1)
    acc = run_query_piece(1, sc_far, far_b, lat_t, acc)
    acc = run_query_piece(1, sc_own, own_b, lat_t, acc)
    got_b, acc = tie((got_b, acc))
    kept_b, send_b = run_halve(kept_b, got_b)
    kept_a, send_b, acc = tie((kept_a, send_b, acc))
    got_b = along(send_b, 1)
    dq = run_query_last(acc, w_uk)
    got_a, dq = tie((got_a, dq))
    kept_a, send_a = run_halve(kept_a, got_a)
    kept_b, send_a = tie((kept_b, send_a))
    got_a = along(send_a, 2)
    kept_b, send_b = run_halve(kept_b, got_b)
    kept_a, send_b = tie((kept_a, send_b))
    got_b = along(send_b, 2)
    (own_a,) = run_halve(kept_a, got_a)
    kept_b, own_a = tie((kept_b, own_a))
    got_a = along(own_a, 2)
    (own_b,) = run_halve(kept_b, got_b)
    own_b, dq = tie((own_b, dq))
    dq = lax.all_to_all(dq, "key", 0, 0, tiled=True)
    own_a, own_b = tie((own_a, own_b))
    got_b = along(own_b, 2)
    own_a = run_join(own_a, got_a)
    own_b, own_a = tie((own_b, own_a))
    got_a = along(own_a, 1)
    own_b = run_join(own_b, got_b)
    own_a, own_b = tie((own_a, own_b))
    got_b = along(own_b, 1)
    own_a = run_join(own_a, got_a)
    own_b, own_a = tie((own_b, own_a))
    far_a, near_a = along(own_a, 0), to_sibling(own_a)
    own_b = run_join(own_b, got_b)
    far_b, near_b = along(own_b, 0), to_sibling(own_b)
    near_parts = ((0, True, 0), (0, False, 0), (1, True, 0), (1, False, 0))
    out = run_settle_near(near_parts, sc_own, (own_a, near_a, own_b, near_b))
    other_a = to_sibling(far_a)
    far_b, out = tie((far_b, out))
    other_b = to_sibling(far_b)
    far_parts = ((0, True, 1), (0, False, 1), (1, True, 1), (1, False, 1))
    pieces = (far_a, other_a, far_b, other_b)
    out, d_queries = run_settle_far(far_parts, sc_own, pieces, dq, out)
    d_latent = out.T

    return (d_queries, d_latent)


def solution(mesh):
    return jax.shard_map(
        shards,
        mesh=mesh,
        in_specs=(
            P(None, "head", None),
            P("head", None, None),
            P("head", None, None),
            P("key", None),
            P(None, "head", None),
            P(),
        ),
        out_specs=(P("key", "head", None), P("key", None)),
        check_vma=False,
    )
```
